32 devices in a mesh: ctx: 2 (over x), ch: 16 (over z, y, core).
Axes of the slice: x: 2, y: 2, z: 4, core: 2. Of those that a mesh axis runs over, the one named last changes fastest.
Arguments:
- first_in: bfloat16 [512, 16384], P('ch', 'ctx'), may hold values from -6 to 6
- second_in: bfloat16 [512, 16384], P('ch', 'ctx'), may hold values from -6 to 6
- third_in: bfloat16 [512, 16384], P('ch', 'ctx'), may hold values from -6 to 6
- grad_heads: bfloat16 [512, 16384], P(None, ('ctx', 'ch')), may hold values from -6 to 6
- residue: float32 [32, 16], P('ch'), may hold values from -1.5 to 1.5
- decay_rate: float32 [32, 16], P('ch'), may hold values from 1.2207031e-05 to 0.1, as said below
- skip_gain: float32 [512], P('ch'), may hold values from -3 to 3
Outputs:
- grad_first: bfloat16 [512, 16384], P('ch', 'ctx')
- grad_second: bfloat16 [512, 16384], P('ch', 'ctx')
- grad_third: bfloat16 [512, 16384], P('ch', 'ctx')
- grad_residue: float32 [32, 16], P('ch')
- grad_skip: float32 [512], P('ch')
The draws below stay inside these ranges and needn't reach their ends.
Inputs may be any that keep to these rules, and one draw needn't show every extreme that they name: `decay_rate`: positive decay rate of each mode.
All inputs are finite; a program needn't handle non-finite values.
Results may differ from the reference program's by a relative error of at most 0.006.
Values may be sent and summed in bfloat16 or wider, within the bound.
A program may use at most 64 MiB of HBM per device.

```python
import jax
import jax.numpy as jnp
from jax import lax

GROUP = 16
NMODE = 16
CHANNELS = 512
NGROUPS = 32
TOKENS = 16384


def draw_decay_rate(key, part):
    pick_key, slow_key, fast_key = jax.random.split(key, 3)
    slow_share = 0.5
    slow_pick = jax.random.uniform(pick_key, (NGROUPS, NMODE), jnp.float32) < slow_share
    slow_rate = jnp.exp(jax.random.uniform(slow_key, (NGROUPS, NMODE), jnp.float32, jnp.log(0.2 / TOKENS), jnp.log(2.0 / TOKENS)))
    fast_rate = jnp.exp(jax.random.uniform(fast_key, (NGROUPS, NMODE), jnp.float32, jnp.log(0.04), jnp.log(0.1)))
    return jnp.where(slow_pick, slow_rate, fast_rate)


def shard_levels(rng, dims, pieces, smallest, high):
    level, own = 1.0, jax.random.fold_in(rng, 6)
    for dim, blocks in pieces:
        draws = jnp.exp(jax.random.uniform(jax.random.fold_in(own, dim), (blocks,), jnp.float32, smallest / len(pieces), high / len(pieces)))
        level = level * jnp.repeat(draws, dims[dim] // blocks).reshape([-1 if axis == dim else 1 for axis in range(len(dims))])
    return level


def gaussian(stream_key, shape, spread, bound, shards=(), kind=jnp.bfloat16):
    drawn = jax.random.normal(stream_key, shape, jnp.float32) * spread
    if len(shards) > 0:
        drawn = shard_levels(stream_key, shape, shards, -0.22, 0.18) * drawn
    return jnp.clip(drawn, min=-bound, max=bound).astype(kind)


def setup_inputs(seed: int = 0) -> dict:
    arg_keys = jax.random.split(jax.random.key(seed), 8)
    first_in = gaussian(arg_keys[0], (CHANNELS, TOKENS), 1.0, 6.0, ((0, 16), (1, 2)))
    second_in = gaussian(arg_keys[1], (CHANNELS, TOKENS), 1.0, 6.0, ((0, 16), (1, 2)))
    third_in = gaussian(arg_keys[2], (CHANNELS, TOKENS), 1.0, 6.0, ((0, 16), (1, 2)))
    grad_heads = gaussian(arg_keys[3], (CHANNELS, TOKENS), 1.0, 6.0, ((1, 32),))
    residue = gaussian(arg_keys[4], (NGROUPS, NMODE), 0.25, 1.5, ((0, 16),), jnp.float32)
    decay_rate = draw_decay_rate(jax.random.fold_in(arg_keys[7], 71), 0)
    skip_gain = gaussian(arg_keys[6], (CHANNELS,), 0.5, 3.0, ((0, 16),), jnp.float32)
    return {"first_in": first_in, "second_in": second_in, "third_in": third_in, "grad_heads": grad_heads, "residue": residue, "decay_rate": decay_rate, "skip_gain": skip_gain}


def reference(first_in, second_in, third_in, grad_heads, residue, decay_rate, skip_gain):
    decay = jnp.repeat(jnp.exp(-decay_rate), GROUP, axis=0)
    weights = jnp.repeat(residue * jnp.sqrt(2.0 * decay_rate), GROUP, axis=0)
    gated = first_in.astype(jnp.float32) * second_in.astype(jnp.float32)
    grad_out = grad_heads.astype(jnp.float32)
    grad_conv = grad_out * third_in.astype(jnp.float32)
    zero_state = jnp.zeros(decay.shape, jnp.float32)

    def forward(carry, column):
        state, running = carry
        gated_t, grad_t = column
        state = decay * state + gated_t[:, None]
        running = running + grad_t[:, None] * state
        return ((state, running), lax.optimization_barrier(jnp.sum(weights * state, axis=1)) + skip_gain * gated_t)
    (final_state, totals), convolved = lax.scan(forward, (zero_state, zero_state), (gated.T, grad_conv.T))
    convolved = convolved.T

    def backward(state, grad_t):
        state = decay * state + grad_t[:, None]
        return (state, lax.optimization_barrier(jnp.sum(weights * state, axis=1)) + skip_gain * grad_t)
    first_state, grad_mixed = lax.scan(backward, zero_state, grad_conv.T, reverse=True)
    grad_mixed = grad_mixed.T
    grad_first = (grad_mixed * second_in.astype(jnp.float32)).astype(jnp.bfloat16)
    grad_second = (grad_mixed * first_in.astype(jnp.float32)).astype(jnp.bfloat16)
    grad_third = (grad_out * convolved).astype(jnp.bfloat16)
    grouped = lax.optimization_barrier(jnp.sum(totals.reshape(NGROUPS, GROUP, NMODE), axis=1))
    grad_residue = jnp.sqrt(2.0 * decay_rate) * grouped / jnp.sqrt(float(GROUP * TOKENS))
    grad_skip = lax.optimization_barrier(jnp.sum(grad_conv * gated, axis=1)) / jnp.sqrt(float(TOKENS))
    return (grad_first, grad_second, grad_third, grad_residue, grad_skip)
```

```python
import functools

import jax
import jax.numpy as jnp
from jax import lax
from jax.experimental import pallas as pl
from jax.experimental.pallas import tpu as pltpu
from jax.sharding import PartitionSpec as P

MESH = pl.DeviceIdType.MESH
EXACT = lax.Precision.HIGHEST
F32 = jnp.float32
BF16 = jnp.bfloat16


def flip(index, bits):
    out, bit = index, 1
    while bit <= bits:
        if bits & bit:
            out = out + bit * (1 - 2 * lax.rem(lax.div(index, bit), 2))
        bit *= 2
    return out


def interleaved(count):
    far, near = list(range(count - 1, count // 2 - 1, -1)), list(range(count // 2 - 1, 0, -1))
    order = []
    for k in range(len(far)):
        order.append(far[k])
        if k < len(near):
            order.append(near[k])
    return order


def dot(a, b, precision=None):
    return jnp.dot(a, b, precision=precision, preferred_element_type=F32)


def dot_nt(a, b):
    return lax.dot_general(a, b, (((1,), (1,)), ((), ())), preferred_element_type=F32)


def dot_tn(a, b):
    return lax.dot_general(a, b, (((0,), (0,)), ((), ())), preferred_element_type=F32)


def kernel(
    dims,
    first_hbm, second_hbm, third_hbm, heads_hbm, residue_ref, decay_ref, skip_ref,
    out_first, out_second, out_third, out_residue, out_skip,
    first, second, third, heads, x_buf, g_buf, conv, stage_first, stage_second, stage_third,
    toep, enter_buf, leave_buf, fwd_pow, bwd_pow, fwd_slots, bwd_slots, sum_slots,
    load_sem, send_sem, recv_sem, fwd_send, fwd_recv, bwd_send, bwd_recv, sum_send, sum_recv,
    third_sem, first_sem, second_sem,
):
    nch, nctx, channels, length, groups, modes, seq_total = dims
    width = channels // groups
    chunk = length // nch
    span = min(256, length)
    spans = length // span
    unit = max(chunk, span)
    per_unit = unit // chunk
    units = length // unit
    unit_spans = unit // span
    me = lax.axis_index("ch")
    me_x = lax.axis_index("ctx")

    loads = [
        pltpu.make_async_copy(src, dst, load_sem.at[k])
        for k, (src, dst) in enumerate(
            ((first_hbm, first), (second_hbm, second), (third_hbm, third))
        )
    ]
    for load in loads:
        load.start()

    def rows_of(index):
        return pl.ds(pl.multiple_of(index * channels, channels), channels)

    def cols_of(index):
        return pl.ds(pl.multiple_of(index * chunk, chunk), chunk)

    own = pltpu.make_async_copy(
        heads_hbm.at[rows_of(me)], heads.at[:, cols_of(me)], recv_sem.at[me]
    )
    own.start()

    barrier = pltpu.get_barrier_semaphore()
    for s in range(1, nch):
        pl.semaphore_signal(barrier, inc=1, device_id={"ch": flip(me, s)}, device_id_type=MESH)
    for k in range(1, nctx):
        pl.semaphore_signal(
            barrier, inc=1, device_id={"ctx": lax.rem(me_x + k, nctx)}, device_id_type=MESH
        )
    pl.semaphore_wait(barrier, nch - 1 + nctx - 1)

    sends = []
    for s in interleaved(nch):
        to = flip(me, s)
        copy = pltpu.make_async_remote_copy(
            src_ref=heads_hbm.at[rows_of(to)],
            dst_ref=heads.at[:, cols_of(me)],
            send_sem=send_sem.at[s],
            recv_sem=recv_sem.at[me],
            device_id={"ch": to},
            device_id_type=MESH,
        )
        copy.start()
        sends.append(copy)

    def spread(slots, send, recv):
        copies = []
        for k in range(1, nctx):
            copy = pltpu.make_async_remote_copy(
                src_ref=slots.at[me_x],
                dst_ref=slots.at[me_x],
                send_sem=send.at[k],
                recv_sem=recv.at[me_x],
                device_id={"ctx": lax.rem(me_x + k, nctx)},
                device_id_type=MESH,
            )
            copy.start()
            copies.append(copy)
        return copies

    def gather(slots, send, recv):
        for k in range(1, nctx):
            at = lax.rem(me_x + k, nctx)
            pltpu.make_async_remote_copy(
                src_ref=slots.at[at],
                dst_ref=slots.at[at],
                send_sem=send.at[k],
                recv_sem=recv.at[at],
                device_id={"ctx": at},
                device_id_type=MESH,
            ).wait_recv()

    def iota(shape, dim):
        return lax.broadcasted_iota(jnp.int32, shape, dim)

    def column(row):
        size = row.shape[1]
        eye = iota((size, size), 0) == iota((size, size), 1)
        return jnp.sum(jnp.where(eye, jnp.broadcast_to(row, (size, size)), 0.0), axis=1, keepdims=True)

    token_row = iota((modes, span), 1).astype(F32)
    token_col = iota((span, modes), 0).astype(F32)
    middle = float(span // 2)
    lower = iota((span, span), 0) >= iota((span, span), 1)
    span_index = lax.div(iota((spans * width, modes), 0), width).astype(F32)
    rate_row, root_row, span_decay, rise, fall, tail, decay_in = [], [], [], [], [], [], []
    fall_col, rise_col = [], []
    for g in range(groups):
        rate = decay_ref[g : g + 1, :]
        root = jnp.sqrt(2.0 * rate)
        weight = residue_ref[g : g + 1, :] * root
        rate_c, weight_c = column(rate), column(weight)
        rate_row.append(rate)
        root_row.append(root)
        span_decay.append(jnp.exp(-rate * span))
        rise.append(weight_c * jnp.exp(-rate_c * token_row))
        fall.append((weight_c * jnp.exp(-rate_c * (span - 1.0 - token_row))).astype(BF16))
        tail.append(jnp.exp(-rate * (span - token_col)).astype(BF16))
        decay_in.append(jnp.exp(-rate * token_col).astype(BF16))
        fall_col.append(jnp.exp(-rate * (token_col - middle)))
        rise_col.append(jnp.exp(rate * (token_col - middle)).astype(BF16))
        rising = jnp.exp(rate_c * (token_row - middle))
        toeplitz = dot(weight * fall_col[g], rising, EXACT)
        toep[g] = jnp.where(lower, toeplitz, 0.0).astype(BF16)
        fwd_pow[g] = jnp.exp(-rate * span * span_index)
        bwd_pow[g] = jnp.exp(-rate * span * (spans - 1.0 - span_index))
    skip_col = column(skip_ref[...])

    loads[0].wait()
    loads[1].wait()

    def gate(n, carry):
        at = pl.ds(pl.multiple_of(n * span, span), span)
        gated = (first[:, at].astype(F32) * second[:, at].astype(F32)).astype(BF16)
        for g in range(groups):
            x_buf[g, pl.ds(pl.multiple_of(n * width, width), width), :] = gated[
                g * width : (g + 1) * width
            ]
        return carry

    lax.fori_loop(0, spans, gate, 0)

    for g in range(groups):
        state = dot(x_buf[g], tail[g])
        run = jnp.zeros((width, modes), F32)
        for n in range(spans):
            at = slice(n * width, (n + 1) * width)
            enter_buf[g, at, :] = run
            run = run * span_decay[g] + state[at]
        fwd_slots[me_x, g * width : (g + 1) * width, :] = run
    fwd_copies = spread(fwd_slots, fwd_send, fwd_recv)
    for g in range(groups):
        conv[g] = dot_nt(x_buf[g], toep[g])
    gather(fwd_slots, fwd_send, fwd_recv)

    def entering(slots, g, before):
        total = jnp.zeros((width, modes), F32)
        for k in range(nctx):
            gap = me_x - 1 - k if before else k - 1 - me_x
            steps = jnp.maximum(gap, 0).astype(F32)
            decayed = slots[k, g * width : (g + 1) * width, :] * jnp.exp(
                -rate_row[g] * length * steps
            )
            total = total + jnp.where(gap >= 0, decayed, 0.0)
        return jnp.concatenate([total] * spans, axis=0)

    for g in range(groups):
        enter = enter_buf[g] + fwd_pow[g] * entering(fwd_slots, g, True)
        enter_buf[g] = enter
        skips = jnp.concatenate([skip_col[g * width : (g + 1) * width]] * spans, axis=0)
        conv[g] = conv[g] + dot(enter, rise[g], EXACT) + skips * x_buf[g].astype(F32)

    loads[2].wait()
    skip_sum = jnp.zeros((channels, span), F32)
    third_copies = []
    order = [0] + interleaved(units) if units > 1 else [0]
    for s in order:
        at_unit = flip(lax.div(me, per_unit), s)
        for q in range(per_unit):
            src = at_unit * per_unit + q
            pltpu.make_async_copy(
                heads_hbm.at[rows_of(0)], heads.at[:, cols_of(src)], recv_sem.at[src]
            ).wait()
        for q in range(unit_spans):
            n = at_unit * unit_spans + q
            cols = pl.ds(pl.multiple_of(n * span, span), span)
            rows = pl.ds(pl.multiple_of(n * width, width), width)
            out_grad = heads[:, cols].astype(F32)
            grad = out_grad * third[:, cols].astype(F32)
            gated = jnp.concatenate([x_buf[g, rows, :] for g in range(groups)], axis=0)
            convolved = jnp.concatenate([conv[g, rows, :] for g in range(groups)], axis=0)
            skip_sum = skip_sum + grad * gated.astype(F32)
            stage_third[:, cols] = (out_grad * convolved).astype(BF16)
            rounded = grad.astype(BF16)
            for g in range(groups):
                g_buf[g, rows, :] = rounded[g * width : (g + 1) * width]
        cols = pl.ds(pl.multiple_of(at_unit * unit, unit), unit)
        copy = pltpu.make_async_copy(
            stage_third.at[:, cols], out_third.at[:, cols], third_sem.at[s]
        )
        copy.start()
        third_copies.append(copy)

    far = []
    for g in range(groups):
        weighted = dot(g_buf[g], decay_in[g])
        far.append(jnp.sum(weighted * enter_buf[g], axis=0, keepdims=True))
        state = weighted * jnp.exp(-rate_row[g])
        run = jnp.zeros((width, modes), F32)
        for n in reversed(range(spans)):
            at = slice(n * width, (n + 1) * width)
            leave_buf[g, at, :] = run
            run = run * span_decay[g] + state[at]
        bwd_slots[me_x, g * width : (g + 1) * width, :] = run
    bwd_copies = spread(bwd_slots, bwd_send, bwd_recv)

    sum_slots[me_x] = jnp.zeros(sum_slots.shape[1:], F32)
    for g in range(groups):
        cross = jnp.where(lower, dot_tn(g_buf[g], x_buf[g]), 0.0).astype(BF16)
        near = jnp.sum(dot(cross, rise_col[g]) * fall_col[g], axis=0, keepdims=True)
        sum_slots[me_x, g : g + 1, 0:modes] = root_row[g] * (near + far[g])
    skip_total = jnp.sum(skip_sum, axis=1, keepdims=True)
    eye = iota((channels, channels), 0) == iota((channels, channels), 1)
    sum_slots[me_x, groups : groups + 1, 0:channels] = jnp.sum(
        jnp.where(eye, jnp.broadcast_to(skip_total, (channels, channels)), 0.0),
        axis=0,
        keepdims=True,
    )
    sum_copies = spread(sum_slots, sum_send, sum_recv)
    for g in range(groups):
        skips = jnp.concatenate([skip_col[g * width : (g + 1) * width]] * spans, axis=0)
        conv[g] = dot(g_buf[g], toep[g]) + skips * g_buf[g].astype(F32)

    gather(bwd_slots, bwd_send, bwd_recv)
    for g in range(groups):
        leave_buf[g] = leave_buf[g] + bwd_pow[g] * entering(bwd_slots, g, False)
    pieces = 4 if spans % 4 == 0 else 1
    piece_spans = spans // pieces
    out_copies = []
    for p in range(pieces):
        for g in range(groups):
            rows = slice(p * piece_spans * width, (p + 1) * piece_spans * width)
            mixed = conv[g, rows, :] + dot(leave_buf[g, rows, :].astype(BF16), fall[g])
            for q in range(piece_spans):
                n = p * piece_spans + q
                part = mixed[q * width : (q + 1) * width]
                at = (slice(g * width, (g + 1) * width), slice(n * span, (n + 1) * span))
                stage_first[at] = (part * second[at].astype(F32)).astype(BF16)
                stage_second[at] = (part * first[at].astype(F32)).astype(BF16)
        cols = pl.ds(p * piece_spans * span, piece_spans * span)
        for stage, out, sem in (
            (stage_first, out_first, first_sem),
            (stage_second, out_second, second_sem),
        ):
            copy = pltpu.make_async_copy(stage.at[:, cols], out.at[:, cols], sem.at[p])
            copy.start()
            out_copies.append(copy)

    gather(sum_slots, sum_send, sum_recv)
    total = sum_slots[0]
    for k in range(1, nctx):
        total = total + sum_slots[k]
    out_residue[...] = total[0:groups, 0:modes] / jnp.sqrt(F32(width * seq_total))
    out_skip[...] = total[groups : groups + 1, 0:channels] / jnp.sqrt(F32(seq_total))

    for copy in sends + fwd_copies + bwd_copies + sum_copies:
        copy.wait_send()
    for copy in third_copies + out_copies:
        copy.wait()


def on_device(nch, nctx, first_in, second_in, third_in, grad_heads, residue, decay_rate, skip_gain):
    channels, length = first_in.shape
    groups, modes = residue.shape
    width = channels // groups
    span = min(256, length)
    spans = length // span
    units = length // max(length // nch, span)
    dims = (nch, nctx, channels, length, groups, modes, length * nctx)
    whole, vmem = pl.BlockSpec(memory_space=pl.ANY), pl.BlockSpec(memory_space=pltpu.VMEM)
    big = jax.ShapeDtypeStruct((channels, length), BF16)
    big_buf = pltpu.VMEM((channels, length), BF16)
    half_buf = pltpu.VMEM((groups, spans * width, span), BF16)
    state_buf = pltpu.VMEM((groups, spans * width, modes), F32)
    slots = pltpu.VMEM((nctx, channels, modes), F32)
    dma = pltpu.SemaphoreType.DMA
    outs = pl.pallas_call(
        functools.partial(kernel, dims),
        out_shape=(
            big, big, big,
            jax.ShapeDtypeStruct((groups, modes), F32),
            jax.ShapeDtypeStruct((1, channels), F32),
        ),
        in_specs=[whole] * 4 + [vmem] * 3,
        out_specs=[whole] * 3 + [vmem] * 2,
        scratch_shapes=[
            big_buf, big_buf, big_buf, big_buf,
            half_buf, half_buf,
            pltpu.VMEM((groups, spans * width, span), F32),
            big_buf, big_buf, big_buf,
            pltpu.VMEM((groups, span, span), BF16),
            state_buf, state_buf, state_buf, state_buf,
            slots, slots,
            pltpu.VMEM((nctx, 8, 128), F32),
            dma((3,)),
            dma((nch,)), dma((nch,)),
            dma((nctx,)), dma((nctx,)), dma((nctx,)), dma((nctx,)), dma((nctx,)), dma((nctx,)),
            dma((units,)), dma((4,)), dma((4,)),
        ],
        compiler_params=pltpu.CompilerParams(
            collective_id=0, has_side_effects=True, vmem_limit_bytes=40 * 1024 * 1024
        ),
        cost_estimate=pl.CostEstimate(
            flops=12 * channels * length * span, bytes_accessed=14 * channels * length,
            transcendentals=0,
        ),
    )(
        first_in, second_in, third_in, grad_heads, residue, decay_rate,
        skip_gain.reshape(1, channels),
    )
    return (*outs[:4], outs[4].reshape(channels))


def solution(mesh):
    return jax.shard_map(
        functools.partial(on_device, mesh.shape["ch"], mesh.shape["ctx"]),
        mesh=mesh,
        in_specs=(
            P("ch", "ctx"),
            P("ch", "ctx"),
            P("ch", "ctx"),
            P(None, ("ctx", "ch")),
            P("ch", None),
            P("ch", None),
            P("ch"),
        ),
        out_specs=(P("ch", "ctx"), P("ch", "ctx"), P("ch", "ctx"), P("ch", None), P("ch")),
        check_vma=False,
    )
```

```python
import functools

import jax
import jax.numpy as jnp
from jax import lax
from jax.experimental import pallas as pl
from jax.experimental.pallas import tpu as pltpu
from jax.sharding import PartitionSpec as P

MESH = pl.DeviceIdType.MESH
EXACT = lax.Precision.HIGHEST
F32 = jnp.float32
BF16 = jnp.bfloat16


def flip(index, bits):
    out, bit = index, 1
    while bit <= bits:
        if bits & bit:
            out = out + bit * (1 - 2 * lax.rem(lax.div(index, bit), 2))
        bit *= 2
    return out


def interleaved(count):
    far, near = list(range(count // 2, count)), list(range(1, count // 2))
    order = []
    for k in range(len(far)):
        order.append(far[k])
        if k < len(near):
            order.append(near[k])
    return order


def dot(a, b, precision=None):
    return jnp.dot(a, b, precision=precision, preferred_element_type=F32)


def dot_nt(a, b):
    return lax.dot_general(a, b, (((1,), (1,)), ((), ())), preferred_element_type=F32)


def dot_tn(a, b):
    return lax.dot_general(a, b, (((0,), (0,)), ((), ())), preferred_element_type=F32)


def kernel(
    dims,
    first_hbm, second_hbm, third_hbm, heads_hbm, residue_hbm, decay_hbm, skip_hbm,
    stage_first, stage_second, stage_third, out_residue, out_skip,
    first, second, third, heads, x_buf, g_buf, conv, cross_buf,
    toep, enter_buf, leave_buf, fwd_pow, bwd_pow, fwd_slots, bwd_slots, sum_slots,
    residue_ref, decay_ref, skip_ref,
    load_sem, send_sem, recv_sem, fwd_send, fwd_recv, bwd_send, bwd_recv, sum_send, sum_recv,
):
    nch, nctx, channels, length, groups, modes, seq_total = dims
    width = channels // groups
    chunk = length // nch
    span = min(256, length)
    spans = length // span
    batches = 4 if nch % 4 == 0 and spans % 4 == 0 else 1
    batch_srcs = nch // batches
    batch_spans = spans // batches
    me = lax.axis_index("ch")
    me_x = lax.axis_index("ctx")

    loads = [
        pltpu.make_async_copy(src, dst, load_sem.at[k])
        for k, (src, dst) in enumerate(
            (
                (first_hbm, first),
                (second_hbm, second),
                (third_hbm, third),
                (residue_hbm, residue_ref),
                (decay_hbm, decay_ref),
                (skip_hbm, skip_ref),
            )
        )
    ]
    for k in (4, 3, 5, 0, 1):
        loads[k].start()

    def rows_of(index):
        return pl.ds(pl.multiple_of(index * channels, channels), channels)

    def cols_of(index):
        return pl.ds(pl.multiple_of(index * chunk, chunk), chunk)

    own = pltpu.make_async_copy(
        heads_hbm.at[rows_of(me)], heads.at[:, cols_of(me)], recv_sem.at[me]
    )

    barrier = pltpu.get_barrier_semaphore()
    for s in range(1, nch):
        pl.semaphore_signal(barrier, inc=1, device_id={"ch": flip(me, s)}, device_id_type=MESH)
    for k in range(1, nctx):
        pl.semaphore_signal(
            barrier, inc=1, device_id={"ctx": lax.rem(me_x + k, nctx)}, device_id_type=MESH
        )
    pl.semaphore_wait(barrier, nch - 1 + nctx - 1)

    sends = []
    for s in interleaved(nch):
        to = flip(me, s)
        copy = pltpu.make_async_remote_copy(
            src_ref=heads_hbm.at[rows_of(to)],
            dst_ref=heads.at[:, cols_of(me)],
            send_sem=send_sem.at[s],
            recv_sem=recv_sem.at[me],
            device_id={"ch": to},
            device_id_type=MESH,
        )
        copy.start()
        sends.append(copy)
    own.start()
    loads[2].start()

    def spread(slots, send, recv):
        copies = []
        for k in range(1, nctx):
            copy = pltpu.make_async_remote_copy(
                src_ref=slots.at[me_x],
                dst_ref=slots.at[me_x],
                send_sem=send.at[k],
                recv_sem=recv.at[me_x],
                device_id={"ctx": lax.rem(me_x + k, nctx)},
                device_id_type=MESH,
            )
            copy.start()
            copies.append(copy)
        return copies

    def gather(slots, send, recv):
        for k in range(1, nctx):
            at = lax.rem(me_x + k, nctx)
            pltpu.make_async_remote_copy(
                src_ref=slots.at[at],
                dst_ref=slots.at[at],
                send_sem=send.at[k],
                recv_sem=recv.at[at],
                device_id={"ctx": at},
                device_id_type=MESH,
            ).wait_recv()

    def iota(shape, dim):
        return lax.broadcasted_iota(jnp.int32, shape, dim)

    def column(row):
        size = row.shape[1]
        eye = iota((size, size), 0) == iota((size, size), 1)
        return jnp.sum(jnp.where(eye, jnp.broadcast_to(row, (size, size)), 0.0), axis=1, keepdims=True)

    for k in (4, 3, 5):
        loads[k].wait()
    token_row = iota((modes, span), 1).astype(F32)
    token_col = iota((span, modes), 0).astype(F32)
    middle = float(span // 2)
    lower = iota((span, span), 0) >= iota((span, span), 1)
    span_index = lax.div(iota((spans * width, modes), 0), width).astype(F32)
    rate_row, root_row, span_decay, rise, fall, tail, decay_in = [], [], [], [], [], [], []
    fall_col, rise_col = [], []
    for g in range(groups):
        rate = decay_ref[g : g + 1, :]
        root = jnp.sqrt(2.0 * rate)
        weight = residue_ref[g : g + 1, :] * root
        rate_c, weight_c = column(rate), column(weight)
        rate_row.append(rate)
        root_row.append(root)
        span_decay.append(jnp.exp(-rate * span))
        rise.append(weight_c * jnp.exp(-rate_c * token_row))
        fall.append((weight_c * jnp.exp(-rate_c * (span - 1.0 - token_row))).astype(BF16))
        tail.append(jnp.exp(-rate * (span - token_col)).astype(BF16))
        decay_in.append(jnp.exp(-rate * token_col).astype(BF16))
        fall_col.append(jnp.exp(-rate * (token_col - middle)))
        rise_col.append(jnp.exp(rate * (token_col - middle)).astype(BF16))
        rising = jnp.exp(rate_c * (token_row - middle))
        toeplitz = dot(weight * fall_col[g], rising, EXACT)
        toep[g] = jnp.where(lower, toeplitz, 0.0).astype(BF16)
        fwd_pow[g] = jnp.exp(-rate * span * span_index)
        bwd_pow[g] = jnp.exp(-rate * span * (spans - 1.0 - span_index))
    skip_col = column(skip_ref[...])

    loads[0].wait()
    loads[1].wait()

    def gate(n, carry):
        at = pl.ds(pl.multiple_of(n * span, span), span)
        gated = (first[:, at].astype(F32) * second[:, at].astype(F32)).astype(BF16)
        for g in range(groups):
            x_buf[g, pl.ds(pl.multiple_of(n * width, width), width), :] = gated[
                g * width : (g + 1) * width
            ]
        return carry

    lax.fori_loop(0, spans, gate, 0)

    for g in range(groups):
        state = dot(x_buf[g], tail[g])
        run = jnp.zeros((width, modes), F32)
        for n in range(spans):
            at = slice(n * width, (n + 1) * width)
            enter_buf[g, at, :] = run
            run = run * span_decay[g] + state[at]
        fwd_slots[me_x, g * width : (g + 1) * width, :] = run
    fwd_copies = spread(fwd_slots, fwd_send, fwd_recv)
    for g in range(groups):
        conv[g] = dot_nt(x_buf[g], toep[g])
    gather(fwd_slots, fwd_send, fwd_recv)

    def entering(slots, g, before):
        total = jnp.zeros((width, modes), F32)
        for k in range(nctx):
            gap = me_x - 1 - k if before else k - 1 - me_x
            steps = jnp.maximum(gap, 0).astype(F32)
            decayed = slots[k, g * width : (g + 1) * width, :] * jnp.exp(
                -rate_row[g] * length * steps
            )
            total = total + jnp.where(gap >= 0, decayed, 0.0)
        return jnp.concatenate([total] * spans, axis=0)

    for g in range(groups):
        enter = enter_buf[g] + fwd_pow[g] * entering(fwd_slots, g, True)
        enter_buf[g] = enter
        skips = jnp.concatenate([skip_col[g * width : (g + 1) * width]] * spans, axis=0)
        conv[g] = conv[g] + dot(enter, rise[g], EXACT) + skips * x_buf[g].astype(F32)

    loads[2].wait()
    batch_rows = batch_spans * width
    skip_sum = jnp.zeros((channels, span), F32)
    far_sum = [jnp.zeros((batch_rows, modes), F32) for _ in range(groups)]
    bwd_sum = [jnp.zeros((batch_rows, modes), F32) for _ in range(groups)]
    bwd_copies = []
    for k in range(batches):
        at_batch = flip(lax.div(me, batch_srcs), k)
        for q in range(batch_srcs):
            src = at_batch * batch_srcs + q
            pltpu.make_async_copy(
                heads_hbm.at[rows_of(0)], heads.at[:, cols_of(src)], recv_sem.at[src]
            ).wait()
        for q in range(batch_spans):
            n = at_batch * batch_spans + q
            cols = pl.ds(pl.multiple_of(n * span, span), span)
            rows = pl.ds(pl.multiple_of(n * width, width), width)
            out_grad = heads[:, cols].astype(F32)
            grad = out_grad * third[:, cols].astype(F32)
            gated = jnp.concatenate([x_buf[g, rows, :] for g in range(groups)], axis=0)
            convolved = jnp.concatenate([conv[g, rows, :] for g in range(groups)], axis=0)
            skip_sum = skip_sum + grad * gated.astype(F32)
            stage_third[:, cols] = (out_grad * convolved).astype(BF16)
            rounded = grad.astype(BF16)
            for g in range(groups):
                g_buf[g, rows, :] = rounded[g * width : (g + 1) * width]
        rows = pl.ds(pl.multiple_of(at_batch * batch_rows, batch_rows), batch_rows)
        for g in range(groups):
            weighted = dot(g_buf[g, rows, :], decay_in[g])
            far_sum[g] = far_sum[g] + weighted * enter_buf[g, rows, :]
            state = weighted * jnp.exp(-rate_row[g])
            leave_buf[g, rows, :] = state
            bwd_sum[g] = bwd_sum[g] + state * fwd_pow[g, rows, :]
        if k == batches - 1:
            for g in range(groups):
                run = bwd_sum[g][0:width]
                for q in range(1, batch_spans):
                    run = run + bwd_sum[g][q * width : (q + 1) * width]
                bwd_slots[me_x, g * width : (g + 1) * width, :] = run
            bwd_copies = spread(bwd_slots, bwd_send, bwd_recv)
        for g in range(groups):
            part = g_buf[g, rows, :]
            skips = jnp.concatenate([skip_col[g * width : (g + 1) * width]] * batch_spans, axis=0)
            conv[g, rows, :] = dot(part, toep[g]) + skips * part.astype(F32)
            cross = dot_tn(part, x_buf[g, rows, :])
            cross_buf[g] = cross if k == 0 else cross_buf[g] + cross

    sum_slots[me_x] = jnp.zeros(sum_slots.shape[1:], F32)
    for g in range(groups):
        cross = jnp.where(lower, cross_buf[g], 0.0).astype(BF16)
        near = jnp.sum(dot(cross, rise_col[g]) * fall_col[g], axis=0, keepdims=True)
        far = jnp.sum(far_sum[g], axis=0, keepdims=True)
        sum_slots[me_x, g : g + 1, 0:modes] = root_row[g] * (near + far)
    skip_total = jnp.sum(skip_sum, axis=1, keepdims=True)
    eye = iota((channels, channels), 0) == iota((channels, channels), 1)
    sum_slots[me_x, groups : groups + 1, 0:channels] = jnp.sum(
        jnp.where(eye, jnp.broadcast_to(skip_total, (channels, channels)), 0.0),
        axis=0,
        keepdims=True,
    )
    sum_copies = spread(sum_slots, sum_send, sum_recv)
    runs = [jnp.zeros((width, modes), F32) for _ in range(groups)]
    for n in reversed(range(spans)):
        at = slice(n * width, (n + 1) * width)
        for g in range(groups):
            state = leave_buf[g, at, :]
            leave_buf[g, at, :] = runs[g]
            runs[g] = runs[g] * span_decay[g] + state

    gather(bwd_slots, bwd_send, bwd_recv)
    for g in range(groups):
        leave_buf[g] = leave_buf[g] + bwd_pow[g] * entering(bwd_slots, g, False)
    pieces = 4 if spans % 4 == 0 else 1
    piece_spans = spans // pieces
    for p in range(pieces):
        for g in range(groups):
            rows = slice(p * piece_spans * width, (p + 1) * piece_spans * width)
            mixed = conv[g, rows, :] + dot(leave_buf[g, rows, :].astype(BF16), fall[g])
            for q in range(piece_spans):
                n = p * piece_spans + q
                part = mixed[q * width : (q + 1) * width]
                at = (slice(g * width, (g + 1) * width), slice(n * span, (n + 1) * span))
                stage_first[at] = (part * second[at].astype(F32)).astype(BF16)
                stage_second[at] = (part * first[at].astype(F32)).astype(BF16)

    gather(sum_slots, sum_send, sum_recv)
    total = sum_slots[0]
    for k in range(1, nctx):
        total = total + sum_slots[k]
    out_residue[...] = total[0:groups, 0:modes] / jnp.sqrt(F32(width * seq_total))
    out_skip[...] = total[groups : groups + 1, 0:channels] / jnp.sqrt(F32(seq_total))

    for copy in sends + fwd_copies + bwd_copies + sum_copies:
        copy.wait_send()


def flush(first, second, third, residue, skip, out_first, out_second, out_third, out_residue, out_skip, sem):
    length = first.shape[1]
    pieces = 4 if length % 512 == 0 else 1
    step = length // pieces
    copies = []
    for p in range(pieces):
        cols = pl.ds(p * step, step)
        for src, dst in ((first, out_first), (second, out_second), (third, out_third)):
            copies.append((src.at[:, cols], dst.at[:, cols]))
    copies += [(residue, out_residue), (skip, out_skip)]
    copies = [pltpu.make_async_copy(src, dst, sem.at[k]) for k, (src, dst) in enumerate(copies)]
    for copy in copies:
        copy.start()
    for copy in copies:
        copy.wait()


def on_device(nch, nctx, first_in, second_in, third_in, grad_heads, residue, decay_rate, skip_gain):
    channels, length = first_in.shape
    groups, modes = residue.shape
    width = channels // groups
    span = min(256, length)
    spans = length // span
    dims = (nch, nctx, channels, length, groups, modes, length * nctx)
    whole, vmem = pl.BlockSpec(memory_space=pltpu.HBM), pl.BlockSpec(memory_space=pltpu.VMEM)
    big = jax.ShapeDtypeStruct((channels, length), BF16)
    big_buf = pltpu.VMEM((channels, length), BF16)
    half_buf = pltpu.VMEM((groups, spans * width, span), BF16)
    state_buf = pltpu.VMEM((groups, spans * width, modes), F32)
    slots = pltpu.VMEM((nctx, channels, modes), F32)
    dma = pltpu.SemaphoreType.DMA
    out_shape = (
        big, big, big,
        jax.ShapeDtypeStruct((groups, modes), F32),
        jax.ShapeDtypeStruct((1, channels), F32),
    )
    outs = pl.pallas_call(
        functools.partial(kernel, dims),
        out_shape=out_shape,
        in_specs=[whole] * 7,
        out_specs=[vmem] * 5,
        scratch_shapes=[
            big_buf, big_buf, big_buf, big_buf,
            half_buf, half_buf,
            pltpu.VMEM((groups, spans * width, span), F32),
            pltpu.VMEM((groups, span, span), F32),
            pltpu.VMEM((groups, span, span), BF16),
            state_buf, state_buf, state_buf, state_buf,
            slots, slots,
            pltpu.VMEM((nctx, 8, 128), F32),
            pltpu.VMEM((groups, modes), F32),
            pltpu.VMEM((groups, modes), F32),
            pltpu.VMEM((1, channels), F32),
            dma((6,)),
            dma((nch,)), dma((nch,)),
            dma((nctx,)), dma((nctx,)), dma((nctx,)), dma((nctx,)), dma((nctx,)), dma((nctx,)),
        ],
        compiler_params=pltpu.CompilerParams(
            collective_id=0, has_side_effects=True, vmem_limit_bytes=32 * 1024 * 1024
        ),
        cost_estimate=pl.CostEstimate(
            flops=12 * channels * length * span, bytes_accessed=14 * channels * length,
            transcendentals=0,
        ),
    )(
        *(
            pltpu.with_memory_space_constraint(part, pltpu.HBM)
            for part in (
                first_in, second_in, third_in, grad_heads, residue, decay_rate,
                skip_gain.reshape(1, channels),
            )
        )
    )
    outs = pl.pallas_call(
        flush,
        out_shape=out_shape,
        in_specs=[vmem] * 5,
        out_specs=[whole] * 5,
        scratch_shapes=[dma((14,))],
        compiler_params=pltpu.CompilerParams(vmem_limit_bytes=8 * 1024 * 1024),
    )(*outs)
    return (*outs[:4], outs[4].reshape(channels))


def solution(mesh):
    return jax.shard_map(
        functools.partial(on_device, mesh.shape["ch"], mesh.shape["ctx"]),
        mesh=mesh,
        in_specs=(
            P("ch", "ctx"),
            P("ch", "ctx"),
            P("ch", "ctx"),
            P(None, ("ctx", "ch")),
            P("ch", None),
            P("ch", None),
            P("ch"),
        ),
        out_specs=(P("ch", "ctx"), P("ch", "ctx"), P("ch", "ctx"), P("ch", None), P("ch")),
        check_vma=False,
    )
```

```python
import functools

import jax
import jax.numpy as jnp
from jax import lax
from jax.experimental import pallas as pl
from jax.experimental.pallas import tpu as pltpu
from jax.sharding import PartitionSpec as P

MESH = pl.DeviceIdType.MESH
EXACT = lax.Precision.HIGHEST
F32 = jnp.float32
BF16 = jnp.bfloat16


def flip(index, bits):
    out, bit = index, 1
    while bit <= bits:
        if bits & bit:
            out = out + bit * (1 - 2 * lax.rem(lax.div(index, bit), 2))
        bit *= 2
    return out


def interleaved(count):
    far, near = list(range(count // 2, count)), list(range(1, count // 2))
    order = []
    for k in range(len(far)):
        order.append(far[k])
        if k < len(near):
            order.append(near[k])
    return order


def dot(a, b, precision=None):
    return jnp.dot(a, b, precision=precision, preferred_element_type=F32)


def dot_nt(a, b):
    return lax.dot_general(a, b, (((1,), (1,)), ((), ())), preferred_element_type=F32)


def dot_tn(a, b):
    return lax.dot_general(a, b, (((0,), (0,)), ((), ())), preferred_element_type=F32)


def kernel(
    dims,
    first_hbm, second_hbm, third_hbm, heads_hbm, residue_hbm, decay_hbm, skip_hbm,
    first, second, stage_third, conv, leave_buf, fall_wide, out_residue, out_skip,
    third, heads, x_buf, g_buf, cross_buf,
    toep, enter_buf, fwd_pow, bwd_pow, fwd_slots, bwd_slots, sum_slots,
    residue_ref, decay_ref, skip_ref,
    load_sem, send_sem, recv_sem, fwd_send, fwd_recv, bwd_send, bwd_recv, sum_send, sum_recv,
):
    nch, nctx, channels, length, groups, modes, seq_total = dims
    width = channels // groups
    chunk = length // nch
    span = min(256, length)
    spans = length // span
    lanes = groups * modes
    unit = max(chunk, span)
    per_unit = unit // chunk
    unit_spans = unit // span
    units = length // unit
    batches = 4 if units % 4 == 0 else 1
    batch_units = units // batches
    batch_spans = spans // batches
    me = lax.axis_index("ch")
    me_x = lax.axis_index("ctx")

    loads = [
        pltpu.make_async_copy(src, dst, load_sem.at[k])
        for k, (src, dst) in enumerate(
            (
                (first_hbm, first),
                (second_hbm, second),
                (third_hbm, third),
                (residue_hbm, residue_ref),
                (decay_hbm, decay_ref),
                (skip_hbm, skip_ref),
            )
        )
    ]
    for k in (4, 3, 5, 0, 1):
        loads[k].start()

    def rows_of(index):
        return pl.ds(pl.multiple_of(index * channels, channels), channels)

    def cols_of(index):
        return pl.ds(pl.multiple_of(index * chunk, chunk), chunk)

    own = pltpu.make_async_copy(
        heads_hbm.at[rows_of(me)], heads.at[:, cols_of(me)], recv_sem.at[me]
    )

    barrier = pltpu.get_barrier_semaphore()
    for s in range(1, nch):
        pl.semaphore_signal(barrier, inc=1, device_id={"ch": flip(me, s)}, device_id_type=MESH)
    for k in range(1, nctx):
        pl.semaphore_signal(
            barrier, inc=1, device_id={"ctx": lax.rem(me_x + k, nctx)}, device_id_type=MESH
        )
    pl.semaphore_wait(barrier, nch - 1 + nctx - 1)

    sends = []
    for s in interleaved(nch):
        to = flip(me, s)
        copy = pltpu.make_async_remote_copy(
            src_ref=heads_hbm.at[rows_of(to)],
            dst_ref=heads.at[:, cols_of(me)],
            send_sem=send_sem.at[s],
            recv_sem=recv_sem.at[me],
            device_id={"ch": to},
            device_id_type=MESH,
        )
        copy.start()
        sends.append(copy)
    own.start()
    loads[2].start()

    def spread(slots, send, recv):
        copies = []
        for k in range(1, nctx):
            copy = pltpu.make_async_remote_copy(
                src_ref=slots.at[me_x],
                dst_ref=slots.at[me_x],
                send_sem=send.at[k],
                recv_sem=recv.at[me_x],
                device_id={"ctx": lax.rem(me_x + k, nctx)},
                device_id_type=MESH,
            )
            copy.start()
            copies.append(copy)
        return copies

    def gather(slots, send, recv):
        for k in range(1, nctx):
            at = lax.rem(me_x + k, nctx)
            pltpu.make_async_remote_copy(
                src_ref=slots.at[at],
                dst_ref=slots.at[at],
                send_sem=send.at[k],
                recv_sem=recv.at[at],
                device_id={"ctx": at},
                device_id_type=MESH,
            ).wait_recv()

    def iota(shape, dim):
        return lax.broadcasted_iota(jnp.int32, shape, dim)

    def column(row):
        size = row.shape[1]
        eye = iota((size, size), 0) == iota((size, size), 1)
        return jnp.sum(jnp.where(eye, jnp.broadcast_to(row, (size, size)), 0.0), axis=1, keepdims=True)

    for k in (4, 3, 5):
        loads[k].wait()
    middle = float(span // 2)
    rate = jnp.concatenate([decay_ref[g : g + 1, :] for g in range(groups)], axis=1)
    weight = jnp.concatenate([residue_ref[g : g + 1, :] for g in range(groups)], axis=1)
    root = jnp.sqrt(2.0 * rate)
    weight = weight * root
    rate_c, weight_c = column(rate), column(weight)
    from_middle = iota((lanes, span), 1).astype(F32) - middle
    falling = weight_c * jnp.exp(-rate_c * from_middle)
    rising = jnp.exp(rate_c * from_middle)
    row_group = lax.div(iota((lanes, span), 0), modes)
    lane_group = lax.div(iota((span, lanes), 1), modes)

    def wide(table):
        return jnp.concatenate(
            [jnp.where(row_group == g, table, 0.0) for g in range(groups)], axis=1
        ).astype(BF16)

    def tall(table):
        return jnp.concatenate(
            [jnp.where(lane_group == g, table, 0.0) for g in range(groups)], axis=0
        ).astype(BF16)

    def split(table):
        high = table.astype(BF16)
        return high, (table - high.astype(F32)).astype(BF16)

    rise_wide = wide(falling * jnp.exp(-rate_c * middle))
    fall_wide[...] = wide(weight_c * rising * jnp.exp(-rate_c * (span - 1.0 - middle)))
    from_middle_col = iota((span, lanes), 0).astype(F32) - middle
    fall_col = jnp.exp(-rate * from_middle_col)
    rise_col = jnp.exp(rate * from_middle_col)
    tail = tall(rise_col * jnp.exp(-rate * (span - middle)))
    decay_in = tall(fall_col * jnp.exp(-rate * middle))
    rise_col = rise_col.astype(BF16)

    loads[0].wait()
    loads[1].wait()

    def gate(n, carry):
        at = pl.ds(pl.multiple_of(n * span, span), span)
        gated = (first[:, at].astype(F32) * second[:, at].astype(F32)).astype(BF16)
        rows = pl.ds(pl.multiple_of(n * width, width), width)
        for g in range(groups):
            x_buf[rows, g * span : (g + 1) * span] = gated[g * width : (g + 1) * width]
        return carry

    lax.fori_loop(0, spans, gate, 0, unroll=8)

    state = dot(x_buf[...], tail)
    span_decay = jnp.exp(-rate * span)
    powers = jnp.exp(-rate * span * iota((spans, lanes), 0).astype(F32))
    run = jnp.zeros((width, lanes), F32)
    for n in range(spans):
        at = slice(n * width, (n + 1) * width)
        enter_buf[at, :] = run
        run = run * span_decay + state[at]
    fwd_slots[me_x] = run
    fwd_copies = spread(fwd_slots, fwd_send, fwd_recv)

    lower = iota((span, span), 0) >= iota((span, span), 1)
    fall_high, fall_low = split(falling)
    rise_high, rise_low = split(rising)
    for g in range(groups):
        at = slice(g * modes, (g + 1) * modes)
        toeplitz = dot_tn(
            jnp.concatenate([fall_high[at], fall_high[at], fall_low[at]], axis=0),
            jnp.concatenate([rise_high[at], rise_low[at], rise_high[at]], axis=0),
        )
        toep[g] = jnp.where(lower, toeplitz, 0.0).astype(BF16)
        at = slice(g * span, (g + 1) * span)
        conv[:, at] = dot_nt(x_buf[:, at], toep[g])
    for n in range(spans):
        power = jnp.broadcast_to(powers[n : n + 1], (width, lanes))
        fwd_pow[n * width : (n + 1) * width, :] = power
        bwd_pow[(spans - 1 - n) * width : (spans - n) * width, :] = power
    skip_wide = jnp.broadcast_to(column(skip_ref[...]), (channels, span))
    gather(fwd_slots, fwd_send, fwd_recv)

    def entering(slots, before):
        total = jnp.zeros((width, lanes), F32)
        for k in range(nctx):
            gap = me_x - 1 - k if before else k - 1 - me_x
            steps = jnp.maximum(gap, 0).astype(F32)
            decayed = slots[k] * jnp.exp(-rate * length * steps)
            total = total + jnp.where(gap >= 0, decayed, 0.0)
        return jnp.concatenate([total] * spans, axis=0)

    enter = enter_buf[...] + fwd_pow[...] * entering(fwd_slots, True)
    enter_buf[...] = enter
    conv[...] = conv[...] + dot(enter.astype(BF16), rise_wide)

    loads[2].wait()
    batch_rows = batch_spans * width
    skip_sum = jnp.zeros((channels, span), F32)
    far_sum = jnp.zeros((batch_rows, lanes), F32)
    bwd_sum = jnp.zeros((batch_rows, lanes), F32)
    bwd_copies = []
    state_decay = jnp.exp(-rate)
    for k in range(batches):
        for p in range(batch_units):
            at_unit = flip(lax.div(me, per_unit), k * batch_units + p)
            for q in range(per_unit):
                src = at_unit * per_unit + q
                pltpu.make_async_copy(
                    heads_hbm.at[rows_of(0)], heads.at[:, cols_of(src)], recv_sem.at[src]
                ).wait()
            for q in range(unit_spans):
                n = at_unit * unit_spans + q
                cols = pl.ds(pl.multiple_of(n * span, span), span)
                rows = pl.ds(pl.multiple_of(n * width, width), width)

                def stacked(ref):
                    return jnp.concatenate(
                        [ref[rows, g * span : (g + 1) * span] for g in range(groups)], axis=0
                    ).astype(F32)

                out_grad = heads[:, cols].astype(F32)
                grad = out_grad * third[:, cols].astype(F32)
                gated = stacked(x_buf)
                skip_sum = skip_sum + grad * gated
                convolved = stacked(conv) + skip_wide * gated
                stage_third[:, cols] = (out_grad * convolved).astype(BF16)
                rounded, direct = grad.astype(BF16), skip_wide * grad
                for g in range(groups):
                    at = slice(g * width, (g + 1) * width)
                    g_buf[rows, g * span : (g + 1) * span] = rounded[at]
                    conv[rows, g * span : (g + 1) * span] = direct[at]
        at_batch = flip(lax.div(me, nch // batches), k)
        rows = pl.ds(pl.multiple_of(at_batch * batch_rows, batch_rows), batch_rows)
        weighted = dot(g_buf[rows, :], decay_in)
        state = weighted * state_decay
        bwd_sum = bwd_sum + state * fwd_pow[rows, :]
        if k == batches - 1:
            run = bwd_sum[0:width]
            for q in range(1, batch_spans):
                run = run + bwd_sum[q * width : (q + 1) * width]
            bwd_slots[me_x] = run
            bwd_copies = spread(bwd_slots, bwd_send, bwd_recv)
        leave_buf[rows, :] = state
        far_sum = far_sum + weighted * enter_buf[rows, :]
        for g in range(groups):
            at = slice(g * span, (g + 1) * span)
            part = g_buf[rows, at]
            conv[rows, at] = conv[rows, at] + dot(part, toep[g])
            cross = dot_tn(part, x_buf[rows, at])
            cross_buf[g] = cross if k == 0 else cross_buf[g] + cross

    filter_sum = jnp.sum(far_sum, axis=0, keepdims=True)
    for g in range(groups):
        cross = jnp.where(lower, cross_buf[g], 0.0).astype(BF16)
        near = jnp.sum(dot(cross, rise_col) * fall_col, axis=0, keepdims=True)
        filter_sum = filter_sum + jnp.where(lane_group[0:1] == g, near, 0.0)
    skip_total = jnp.sum(skip_sum, axis=1, keepdims=True)
    eye = iota((channels, channels), 0) == iota((channels, channels), 1)
    sum_slots[me_x] = jnp.zeros(sum_slots.shape[1:], F32)
    sum_slots[me_x, 0:1, 0:lanes] = root * filter_sum
    sum_slots[me_x, 1:2, 0:channels] = jnp.sum(
        jnp.where(eye, jnp.broadcast_to(skip_total, (channels, channels)), 0.0),
        axis=0,
        keepdims=True,
    )
    sum_copies = spread(sum_slots, sum_send, sum_recv)
    run = jnp.zeros((width, lanes), F32)
    for n in reversed(range(spans)):
        at = slice(n * width, (n + 1) * width)
        state = leave_buf[at, :]
        leave_buf[at, :] = run
        run = run * span_decay + state

    gather(bwd_slots, bwd_send, bwd_recv)
    leave_buf[...] = leave_buf[...] + bwd_pow[...] * entering(bwd_slots, False)

    gather(sum_slots, sum_send, sum_recv)
    total = sum_slots[0]
    for k in range(1, nctx):
        total = total + sum_slots[k]
    for g in range(groups):
        out_residue[g : g + 1, :] = total[0:1, g * modes : (g + 1) * modes] / jnp.sqrt(
            F32(width * seq_total)
        )
    out_skip[...] = total[1:2, 0:channels] / jnp.sqrt(F32(seq_total))

    for copy in sends + fwd_copies + bwd_copies + sum_copies:
        copy.wait_send()


def finish(
    width,
    first, second, third, conv, leave, fall_wide, residue, skip,
    out_first, out_second, out_third, out_residue, out_skip,
    stage_first, stage_second, sem,
):
    channels, length = first.shape
    groups = channels // width
    span = conv.shape[1] // groups
    spans = length // span
    pieces = 4 if spans % 4 == 0 else 1
    piece_spans = spans // pieces
    copies = []

    def send(src, dst):
        copies.append(pltpu.make_async_copy(src, dst, sem.at[len(copies)]))
        copies[-1].start()

    for p in range(pieces):
        cols = pl.ds(p * piece_spans * span, piece_spans * span)
        send(third.at[:, cols], out_third.at[:, cols])
    send(residue, out_residue)
    send(skip, out_skip)
    for p in range(pieces):
        rows = slice(p * piece_spans * width, (p + 1) * piece_spans * width)
        for g in range(groups):
            lanes = slice(g * span, (g + 1) * span)
            mixed = conv[rows, lanes] + dot(leave[rows, :].astype(BF16), fall_wide[:, lanes])
            for q in range(piece_spans):
                n = p * piece_spans + q
                part = mixed[q * width : (q + 1) * width]
                at = (slice(g * width, (g + 1) * width), slice(n * span, (n + 1) * span))
                stage_first[at] = (part * second[at].astype(F32)).astype(BF16)
                stage_second[at] = (part * first[at].astype(F32)).astype(BF16)
        cols = pl.ds(p * piece_spans * span, piece_spans * span)
        send(stage_first.at[:, cols], out_first.at[:, cols])
        send(stage_second.at[:, cols], out_second.at[:, cols])
    for copy in copies:
        copy.wait()


def on_device(nch, nctx, first_in, second_in, third_in, grad_heads, residue, decay_rate, skip_gain):
    channels, length = first_in.shape
    groups, modes = residue.shape
    width = channels // groups
    span = min(256, length)
    rows = length // span * width
    lanes = groups * modes
    dims = (nch, nctx, channels, length, groups, modes, length * nctx)
    whole, vmem = pl.BlockSpec(memory_space=pltpu.HBM), pl.BlockSpec(memory_space=pltpu.VMEM)
    big = jax.ShapeDtypeStruct((channels, length), BF16)
    small = (
        jax.ShapeDtypeStruct((groups, modes), F32),
        jax.ShapeDtypeStruct((1, channels), F32),
    )
    big_buf = pltpu.VMEM((channels, length), BF16)
    half_buf = pltpu.VMEM((rows, groups * span), BF16)
    state_buf = pltpu.VMEM((rows, lanes), F32)
    slots = pltpu.VMEM((nctx, width, lanes), F32)
    dma = pltpu.SemaphoreType.DMA
    outs = pl.pallas_call(
        functools.partial(kernel, dims),
        out_shape=(
            big, big, big,
            jax.ShapeDtypeStruct((rows, groups * span), F32),
            jax.ShapeDtypeStruct((rows, lanes), F32),
            jax.ShapeDtypeStruct((lanes, groups * span), BF16),
            *small,
        ),
        in_specs=[whole] * 7,
        out_specs=[vmem] * 8,
        scratch_shapes=[
            big_buf, big_buf,
            half_buf, half_buf,
            pltpu.VMEM((groups, span, span), F32),
            pltpu.VMEM((groups, span, span), BF16),
            state_buf, state_buf, state_buf,
            slots, slots,
            pltpu.VMEM((nctx, 8, 128), F32),
            pltpu.VMEM((groups, modes), F32),
            pltpu.VMEM((groups, modes), F32),
            pltpu.VMEM((1, channels), F32),
            dma((6,)),
            dma((nch,)), dma((nch,)),
            dma((nctx,)), dma((nctx,)), dma((nctx,)), dma((nctx,)), dma((nctx,)), dma((nctx,)),
        ],
        compiler_params=pltpu.CompilerParams(
            collective_id=0, has_side_effects=True, vmem_limit_bytes=32 * 1024 * 1024
        ),
        cost_estimate=pl.CostEstimate(
            flops=12 * channels * length * span, bytes_accessed=14 * channels * length,
            transcendentals=0,
        ),
    )(
        *(
            pltpu.with_memory_space_constraint(part, pltpu.HBM)
            for part in (
                first_in, second_in, third_in, grad_heads, residue, decay_rate,
                skip_gain.reshape(1, channels),
            )
        )
    )
    outs = pl.pallas_call(
        functools.partial(finish, width),
        out_shape=(big, big, big, *small),
        in_specs=[vmem] * 8,
        out_specs=[whole] * 5,
        scratch_shapes=[big_buf, big_buf, dma((14,))],
        compiler_params=pltpu.CompilerParams(vmem_limit_bytes=16 * 1024 * 1024),
    )(*outs)
    return (*outs[:4], outs[4].reshape(channels))


def solution(mesh):
    return jax.shard_map(
        functools.partial(on_device, mesh.shape["ch"], mesh.shape["ctx"]),
        mesh=mesh,
        in_specs=(
            P("ch", "ctx"),
            P("ch", "ctx"),
            P("ch", "ctx"),
            P(None, ("ctx", "ch")),
            P("ch", None),
            P("ch", None),
            P("ch"),
        ),
        out_specs=(P("ch", "ctx"), P("ch", "ctx"), P("ch", "ctx"), P("ch", None), P("ch")),
        check_vma=False,
    )
```

```python
import functools

import jax
import jax.numpy as jnp
from jax import lax
from jax.experimental import pallas as pl
from jax.experimental.pallas import tpu as pltpu
from jax.sharding import PartitionSpec as P

MESH = pl.DeviceIdType.MESH
EXACT = lax.Precision.HIGHEST
F32 = jnp.float32
BF16 = jnp.bfloat16


def flip(index, bits):
    out, bit = index, 1
    while bit <= bits:
        if bits & bit:
            out = out + bit * (1 - 2 * lax.rem(lax.div(index, bit), 2))
        bit *= 2
    return out


def far_first(count):
    half, quarter = count // 2, max(count // 4, 1)
    return [*range(half, count), *range(quarter, half), *range(1, quarter)]


def dot(a, b, precision=None):
    return jnp.dot(a, b, precision=precision, preferred_element_type=F32)


def dot_nt(a, b):
    return lax.dot_general(a, b, (((1,), (1,)), ((), ())), preferred_element_type=F32)


def dot_tn(a, b):
    return lax.dot_general(a, b, (((0,), (0,)), ((), ())), preferred_element_type=F32)


def kernel(
    dims,
    first_hbm, second_hbm, third_hbm, heads_hbm, residue_hbm, decay_hbm, skip_hbm,
    first, second, stage_third, conv, leave_buf, fall_wide, out_residue, out_skip,
    third, heads, x_buf, g_buf, cross_buf,
    toep, enter_buf, fwd_pow, bwd_pow, fwd_slots, bwd_slots, sum_slots,
    residue_ref, decay_ref, skip_ref,
    load_sem, send_sem, recv_sem, fwd_send, fwd_recv, bwd_send, bwd_recv, sum_send, sum_recv,
):
    nch, nctx, channels, length, groups, modes, seq_total = dims
    width = channels // groups
    chunk = length // nch
    span = min(256, length)
    spans = length // span
    lanes = groups * modes
    unit = max(chunk, span)
    per_unit = unit // chunk
    unit_spans = unit // span
    units = length // unit
    batches = 4 if units % 4 == 0 else 1
    batch_units = units // batches
    batch_spans = spans // batches
    me = lax.axis_index("ch")
    me_x = lax.axis_index("ctx")

    loads = [
        pltpu.make_async_copy(src, dst, load_sem.at[k])
        for k, (src, dst) in enumerate(
            (
                (first_hbm, first),
                (second_hbm, second),
                (third_hbm, third),
                (residue_hbm, residue_ref),
                (decay_hbm, decay_ref),
                (skip_hbm, skip_ref),
            )
        )
    ]
    for k in (4, 3, 5, 0, 1):
        loads[k].start()

    def rows_of(index):
        return pl.ds(pl.multiple_of(index * channels, channels), channels)

    def cols_of(index):
        return pl.ds(pl.multiple_of(index * chunk, chunk), chunk)

    own = pltpu.make_async_copy(
        heads_hbm.at[rows_of(me)], heads.at[:, cols_of(me)], recv_sem.at[me]
    )

    barrier = pltpu.get_barrier_semaphore()
    for s in range(1, nch):
        pl.semaphore_signal(barrier, inc=1, device_id={"ch": flip(me, s)}, device_id_type=MESH)
    for k in range(1, nctx):
        pl.semaphore_signal(
            barrier, inc=1, device_id={"ctx": lax.rem(me_x + k, nctx)}, device_id_type=MESH
        )
    pl.semaphore_wait(barrier, nch - 1 + nctx - 1)

    sends = []
    for s in far_first(nch):
        to = flip(me, s)
        copy = pltpu.make_async_remote_copy(
            src_ref=heads_hbm.at[rows_of(to)],
            dst_ref=heads.at[:, cols_of(me)],
            send_sem=send_sem.at[s],
            recv_sem=recv_sem.at[me],
            device_id={"ch": to},
            device_id_type=MESH,
        )
        copy.start()
        sends.append(copy)
    own.start()
    loads[2].start()

    def spread(slots, send, recv):
        copies = []
        for k in range(1, nctx):
            copy = pltpu.make_async_remote_copy(
                src_ref=slots.at[me_x],
                dst_ref=slots.at[me_x],
                send_sem=send.at[k],
                recv_sem=recv.at[me_x],
                device_id={"ctx": lax.rem(me_x + k, nctx)},
                device_id_type=MESH,
            )
            copy.start()
            copies.append(copy)
        return copies

    def gather(slots, send, recv):
        for k in range(1, nctx):
            at = lax.rem(me_x + k, nctx)
            pltpu.make_async_remote_copy(
                src_ref=slots.at[at],
                dst_ref=slots.at[at],
                send_sem=send.at[k],
                recv_sem=recv.at[at],
                device_id={"ctx": at},
                device_id_type=MESH,
            ).wait_recv()

    def iota(shape, dim):
        return lax.broadcasted_iota(jnp.int32, shape, dim)

    def column(row):
        size = row.shape[1]
        eye = iota((size, size), 0) == iota((size, size), 1)
        return jnp.sum(jnp.where(eye, jnp.broadcast_to(row, (size, size)), 0.0), axis=1, keepdims=True)

    for k in (4, 3, 5):
        loads[k].wait()
    middle = float(span // 2)
    rate = jnp.concatenate([decay_ref[g : g + 1, :] for g in range(groups)], axis=1)
    weight = jnp.concatenate([residue_ref[g : g + 1, :] for g in range(groups)], axis=1)
    root = jnp.sqrt(2.0 * rate)
    weight = weight * root
    rate_c, weight_c = column(rate), column(weight)
    from_middle = iota((lanes, span), 1).astype(F32) - middle
    falling = weight_c * jnp.exp(-rate_c * from_middle)
    rising = jnp.exp(rate_c * from_middle)
    row_group = lax.div(iota((lanes, span), 0), modes)
    lane_group = lax.div(iota((span, lanes), 1), modes)

    def wide(table):
        return jnp.concatenate(
            [jnp.where(row_group == g, table, 0.0) for g in range(groups)], axis=1
        ).astype(BF16)

    def tall(table):
        return jnp.concatenate(
            [jnp.where(lane_group == g, table, 0.0) for g in range(groups)], axis=0
        ).astype(BF16)

    def split(table):
        high = table.astype(BF16)
        return high, (table - high.astype(F32)).astype(BF16)

    rise_wide = wide(falling * jnp.exp(-rate_c * middle))
    fall_wide[...] = wide(weight_c * rising * jnp.exp(-rate_c * (span - 1.0 - middle)))
    from_middle_col = iota((span, lanes), 0).astype(F32) - middle
    fall_col = jnp.exp(-rate * from_middle_col)
    rise_col = jnp.exp(rate * from_middle_col)
    tail = tall(rise_col * jnp.exp(-rate * (span - middle)))
    decay_in = tall(fall_col * jnp.exp(-rate * middle))
    rise_col = rise_col.astype(BF16)

    loads[0].wait()
    loads[1].wait()

    def gate(n, carry):
        at = pl.ds(pl.multiple_of(n * span, span), span)
        gated = (first[:, at].astype(F32) * second[:, at].astype(F32)).astype(BF16)
        rows = pl.ds(pl.multiple_of(n * width, width), width)
        for g in range(groups):
            x_buf[rows, g * span : (g + 1) * span] = gated[g * width : (g + 1) * width]
        return carry

    lax.fori_loop(0, spans, gate, 0, unroll=8)

    state = dot(x_buf[...], tail)
    span_decay = jnp.exp(-rate * span)
    powers = jnp.exp(-rate * span * iota((spans, lanes), 0).astype(F32))
    run = jnp.zeros((width, lanes), F32)
    for n in range(spans):
        at = slice(n * width, (n + 1) * width)
        enter_buf[at, :] = run
        run = run * span_decay + state[at]
    fwd_slots[me_x] = run
    fwd_copies = spread(fwd_slots, fwd_send, fwd_recv)

    lower = iota((span, span), 0) >= iota((span, span), 1)
    fall_high, fall_low = split(falling)
    rise_high, rise_low = split(rising)
    for g in range(groups):
        at = slice(g * modes, (g + 1) * modes)
        toeplitz = dot_tn(
            jnp.concatenate([fall_high[at], fall_high[at], fall_low[at]], axis=0),
            jnp.concatenate([rise_high[at], rise_low[at], rise_high[at]], axis=0),
        )
        toep[g] = jnp.where(lower, toeplitz, 0.0).astype(BF16)
        at = slice(g * span, (g + 1) * span)
        conv[:, at] = dot_nt(x_buf[:, at], toep[g])
    for n in range(spans):
        power = jnp.broadcast_to(powers[n : n + 1], (width, lanes))
        fwd_pow[n * width : (n + 1) * width, :] = power
        bwd_pow[(spans - 1 - n) * width : (spans - n) * width, :] = power
    skip_wide = jnp.broadcast_to(column(skip_ref[...]), (channels, span))
    gather(fwd_slots, fwd_send, fwd_recv)

    def entering(slots, before):
        total = jnp.zeros((width, lanes), F32)
        for k in range(nctx):
            gap = me_x - 1 - k if before else k - 1 - me_x
            steps = jnp.maximum(gap, 0).astype(F32)
            decayed = slots[k] * jnp.exp(-rate * length * steps)
            total = total + jnp.where(gap >= 0, decayed, 0.0)
        return jnp.concatenate([total] * spans, axis=0)

    enter = enter_buf[...] + fwd_pow[...] * entering(fwd_slots, True)
    enter_buf[...] = enter
    conv[...] = conv[...] + dot(enter.astype(BF16), rise_wide)

    loads[2].wait()
    batch_rows = batch_spans * width
    skip_sum = jnp.zeros((channels, span), F32)
    far_sum = jnp.zeros((batch_rows, lanes), F32)
    bwd_sum = jnp.zeros((batch_rows, lanes), F32)
    bwd_copies = []
    state_decay = jnp.exp(-rate)
    for k in range(batches):
        for p in range(batch_units):
            at_unit = flip(lax.div(me, per_unit), k * batch_units + p)
            for q in range(per_unit):
                src = at_unit * per_unit + q
                pltpu.make_async_copy(
                    heads_hbm.at[rows_of(0)], heads.at[:, cols_of(src)], recv_sem.at[src]
                ).wait()
            for q in range(unit_spans):
                n = at_unit * unit_spans + q
                cols = pl.ds(pl.multiple_of(n * span, span), span)
                rows = pl.ds(pl.multiple_of(n * width, width), width)

                def stacked(ref):
                    return jnp.concatenate(
                        [ref[rows, g * span : (g + 1) * span] for g in range(groups)], axis=0
                    ).astype(F32)

                out_grad = heads[:, cols].astype(F32)
                grad = out_grad * third[:, cols].astype(F32)
                gated = stacked(x_buf)
                skip_sum = skip_sum + grad * gated
                convolved = stacked(conv) + skip_wide * gated
                stage_third[:, cols] = (out_grad * convolved).astype(BF16)
                rounded, direct = grad.astype(BF16), skip_wide * grad
                for g in range(groups):
                    at = slice(g * width, (g + 1) * width)
                    g_buf[rows, g * span : (g + 1) * span] = rounded[at]
                    conv[rows, g * span : (g + 1) * span] = direct[at]
        at_batch = flip(lax.div(me, nch // batches), k)
        rows = pl.ds(pl.multiple_of(at_batch * batch_rows, batch_rows), batch_rows)
        weighted = dot(g_buf[rows, :], decay_in)
        state = weighted * state_decay
        bwd_sum = bwd_sum + state * fwd_pow[rows, :]
        if k == batches - 1:
            run = bwd_sum[0:width]
            for q in range(1, batch_spans):
                run = run + bwd_sum[q * width : (q + 1) * width]
            bwd_slots[me_x] = run
            bwd_copies = spread(bwd_slots, bwd_send, bwd_recv)
        leave_buf[rows, :] = state
        far_sum = far_sum + weighted * enter_buf[rows, :]
        for g in range(groups):
            at = slice(g * span, (g + 1) * span)
            part = g_buf[rows, at]
            conv[rows, at] = conv[rows, at] + dot(part, toep[g])
            cross = dot_tn(part, x_buf[rows, at])
            cross_buf[g] = cross if k == 0 else cross_buf[g] + cross

    filter_sum = jnp.sum(far_sum, axis=0, keepdims=True)
    for g in range(groups):
        cross = jnp.where(lower, cross_buf[g], 0.0).astype(BF16)
        near = jnp.sum(dot(cross, rise_col) * fall_col, axis=0, keepdims=True)
        filter_sum = filter_sum + jnp.where(lane_group[0:1] == g, near, 0.0)
    skip_total = jnp.sum(skip_sum, axis=1, keepdims=True)
    eye = iota((channels, channels), 0) == iota((channels, channels), 1)
    sum_slots[me_x] = jnp.zeros(sum_slots.shape[1:], F32)
    sum_slots[me_x, 0:1, 0:lanes] = root * filter_sum
    sum_slots[me_x, 1:2, 0:channels] = jnp.sum(
        jnp.where(eye, jnp.broadcast_to(skip_total, (channels, channels)), 0.0),
        axis=0,
        keepdims=True,
    )
    sum_copies = spread(sum_slots, sum_send, sum_recv)
    run = jnp.zeros((width, lanes), F32)
    for n in reversed(range(spans)):
        at = slice(n * width, (n + 1) * width)
        state = leave_buf[at, :]
        leave_buf[at, :] = run
        run = run * span_decay + state

    gather(bwd_slots, bwd_send, bwd_recv)
    leave_buf[...] = leave_buf[...] + bwd_pow[...] * entering(bwd_slots, False)

    gather(sum_slots, sum_send, sum_recv)
    total = sum_slots[0]
    for k in range(1, nctx):
        total = total + sum_slots[k]
    for g in range(groups):
        out_residue[g : g + 1, :] = total[0:1, g * modes : (g + 1) * modes] / jnp.sqrt(
            F32(width * seq_total)
        )
    out_skip[...] = total[1:2, 0:channels] / jnp.sqrt(F32(seq_total))

    for copy in sends + fwd_copies + bwd_copies + sum_copies:
        copy.wait_send()


def finish(
    width,
    first, second, third, conv, leave, fall_wide, residue, skip,
    out_first, out_second, out_third, out_residue, out_skip,
    stage_first, stage_second, sem,
):
    channels, length = first.shape
    groups = channels // width
    span = conv.shape[1] // groups
    spans = length // span
    pieces = 4 if spans % 4 == 0 else 1
    piece_spans = spans // pieces
    copies = []

    def send(src, dst):
        copies.append(pltpu.make_async_copy(src, dst, sem.at[len(copies)]))
        copies[-1].start()

    for p in range(pieces):
        cols = pl.ds(p * piece_spans * span, piece_spans * span)
        send(third.at[:, cols], out_third.at[:, cols])
    send(residue, out_residue)
    send(skip, out_skip)
    for p in range(pieces):
        rows = slice(p * piece_spans * width, (p + 1) * piece_spans * width)
        for g in range(groups):
            lanes = slice(g * span, (g + 1) * span)
            mixed = conv[rows, lanes] + dot(leave[rows, :].astype(BF16), fall_wide[:, lanes])
            for q in range(piece_spans):
                n = p * piece_spans + q
                part = mixed[q * width : (q + 1) * width]
                at = (slice(g * width, (g + 1) * width), slice(n * span, (n + 1) * span))
                stage_first[at] = (part * second[at].astype(F32)).astype(BF16)
                stage_second[at] = (part * first[at].astype(F32)).astype(BF16)
        cols = pl.ds(p * piece_spans * span, piece_spans * span)
        send(stage_first.at[:, cols], out_first.at[:, cols])
        send(stage_second.at[:, cols], out_second.at[:, cols])
    for copy in copies:
        copy.wait()


def on_device(nch, nctx, first_in, second_in, third_in, grad_heads, residue, decay_rate, skip_gain):
    channels, length = first_in.shape
    groups, modes = residue.shape
    width = channels // groups
    span = min(256, length)
    rows = length // span * width
    lanes = groups * modes
    dims = (nch, nctx, channels, length, groups, modes, length * nctx)
    whole, vmem = pl.BlockSpec(memory_space=pltpu.HBM), pl.BlockSpec(memory_space=pltpu.VMEM)
    big = jax.ShapeDtypeStruct((channels, length), BF16)
    small = (
        jax.ShapeDtypeStruct((groups, modes), F32),
        jax.ShapeDtypeStruct((1, channels), F32),
    )
    big_buf = pltpu.VMEM((channels, length), BF16)
    half_buf = pltpu.VMEM((rows, groups * span), BF16)
    state_buf = pltpu.VMEM((rows, lanes), F32)
    slots = pltpu.VMEM((nctx, width, lanes), F32)
    dma = pltpu.SemaphoreType.DMA
    outs = pl.pallas_call(
        functools.partial(kernel, dims),
        out_shape=(
            big, big, big,
            jax.ShapeDtypeStruct((rows, groups * span), F32),
            jax.ShapeDtypeStruct((rows, lanes), F32),
            jax.ShapeDtypeStruct((lanes, groups * span), BF16),
            *small,
        ),
        in_specs=[whole] * 7,
        out_specs=[vmem] * 8,
        scratch_shapes=[
            big_buf, big_buf,
            half_buf, half_buf,
            pltpu.VMEM((groups, span, span), F32),
            pltpu.VMEM((groups, span, span), BF16),
            state_buf, state_buf, state_buf,
            slots, slots,
            pltpu.VMEM((nctx, 8, 128), F32),
            pltpu.VMEM((groups, modes), F32),
            pltpu.VMEM((groups, modes), F32),
            pltpu.VMEM((1, channels), F32),
            dma((6,)),
            dma((nch,)), dma((nch,)),
            dma((nctx,)), dma((nctx,)), dma((nctx,)), dma((nctx,)), dma((nctx,)), dma((nctx,)),
        ],
        compiler_params=pltpu.CompilerParams(
            collective_id=0, has_side_effects=True, vmem_limit_bytes=32 * 1024 * 1024
        ),
        cost_estimate=pl.CostEstimate(
            flops=12 * channels * length * span, bytes_accessed=14 * channels * length,
            transcendentals=0,
        ),
    )(
        *(
            pltpu.with_memory_space_constraint(part, pltpu.HBM)
            for part in (
                first_in, second_in, third_in, grad_heads, residue, decay_rate,
                skip_gain.reshape(1, channels),
            )
        )
    )
    outs = pl.pallas_call(
        functools.partial(finish, width),
        out_shape=(big, big, big, *small),
        in_specs=[vmem] * 8,
        out_specs=[whole] * 5,
        scratch_shapes=[big_buf, big_buf, dma((14,))],
        compiler_params=pltpu.CompilerParams(vmem_limit_bytes=16 * 1024 * 1024),
    )(*outs)
    return (*outs[:4], outs[4].reshape(channels))


def solution(mesh):
    return jax.shard_map(
        functools.partial(on_device, mesh.shape["ch"], mesh.shape["ctx"]),
        mesh=mesh,
        in_specs=(
            P("ch", "ctx"),
            P("ch", "ctx"),
            P("ch", "ctx"),
            P(None, ("ctx", "ch")),
            P("ch", None),
            P("ch", None),
            P("ch"),
        ),
        out_specs=(P("ch", "ctx"), P("ch", "ctx"), P("ch", "ctx"), P("ch", None), P("ch")),
        check_vma=False,
    )
```

```python
import functools

import jax
import jax.numpy as jnp
from jax import lax
from jax.experimental import pallas as pl
from jax.experimental.pallas import tpu as pltpu
from jax.sharding import PartitionSpec as P

MESH = pl.DeviceIdType.MESH
EXACT = lax.Precision.HIGHEST
F32 = jnp.float32
BF16 = jnp.bfloat16


def flip(index, bits):
    out, bit = index, 1
    while bit <= bits:
        if bits & bit:
            out = out + bit * (1 - 2 * lax.rem(lax.div(index, bit), 2))
        bit *= 2
    return out


def dot(a, b, precision=None):
    return jnp.dot(a, b, precision=precision, preferred_element_type=F32)


def dot_nt(a, b):
    return lax.dot_general(a, b, (((1,), (1,)), ((), ())), preferred_element_type=F32)


def dot_tn(a, b):
    return lax.dot_general(a, b, (((0,), (0,)), ((), ())), preferred_element_type=F32)


def kernel(
    dims,
    first_hbm, second_hbm, third_hbm, heads_hbm, residue_hbm, decay_hbm, skip_hbm,
    first, second, stage_third, conv, leave_buf, fall_wide, out_residue, out_skip,
    third, heads, x_buf, g_buf, cross_buf,
    toep, enter_buf, fwd_pow, bwd_pow, fwd_slots, bwd_slots, sum_slots,
    residue_ref, decay_ref, skip_ref,
    load_sem, send_sem, recv_sem, fwd_send, fwd_recv, bwd_send, bwd_recv, sum_send, sum_recv,
):
    nch, nctx, channels, length, groups, modes, seq_total = dims
    width = channels // groups
    chunk = length // nch
    span = min(256, length)
    spans = length // span
    lanes = groups * modes
    unit = max(chunk, span)
    per_unit = unit // chunk
    unit_spans = unit // span
    units = length // unit
    batches = [(units, 0)]
    if units % 8 == 0:
        batches = [(units // 4, k) for k in range(3)] + [(units // 8, 6), (units // 8, 7)]
    me = lax.axis_index("ch")
    me_x = lax.axis_index("ctx")

    loads = [
        pltpu.make_async_copy(src, dst, load_sem.at[k])
        for k, (src, dst) in enumerate(
            (
                (first_hbm, first),
                (second_hbm, second),
                (third_hbm, third),
                (residue_hbm, residue_ref),
                (decay_hbm, decay_ref),
                (skip_hbm, skip_ref),
            )
        )
    ]
    def rows_of(index):
        return pl.ds(pl.multiple_of(index * channels, channels), channels)

    def cols_of(index):
        return pl.ds(pl.multiple_of(index * chunk, chunk), chunk)

    own = pltpu.make_async_copy(
        heads_hbm.at[rows_of(me)], heads.at[:, cols_of(me)], recv_sem.at[me]
    )

    barrier = pltpu.get_barrier_semaphore()
    for s in range(1, nch):
        pl.semaphore_signal(barrier, inc=1, device_id={"ch": flip(me, s)}, device_id_type=MESH)
    for k in range(1, nctx):
        pl.semaphore_signal(
            barrier, inc=1, device_id={"ctx": lax.rem(me_x + k, nctx)}, device_id_type=MESH
        )
    for k in (4, 3, 5, 0, 1):
        loads[k].start()
    pl.semaphore_wait(barrier, nch - 1 + nctx - 1)

    sends = []

    def send_to(places):
        for s in places:
            to = flip(me, s)
            copy = pltpu.make_async_remote_copy(
                src_ref=heads_hbm.at[rows_of(to)],
                dst_ref=heads.at[:, cols_of(me)],
                send_sem=send_sem.at[s],
                recv_sem=recv_sem.at[me],
                device_id={"ch": to},
                device_id_type=MESH,
            )
            copy.start()
            sends.append(copy)

    first_step, second_step = nch * 3 // 4, nch * 7 // 8
    send_to(range(nch // 2, first_step))
    send_to(range(1, nch // 2))
    own.start()
    loads[2].start()

    def spread(slots, send, recv):
        copies = []
        for k in range(1, nctx):
            copy = pltpu.make_async_remote_copy(
                src_ref=slots.at[me_x],
                dst_ref=slots.at[me_x],
                send_sem=send.at[k],
                recv_sem=recv.at[me_x],
                device_id={"ctx": lax.rem(me_x + k, nctx)},
                device_id_type=MESH,
            )
            copy.start()
            copies.append(copy)
        return copies

    def gather(slots, send, recv):
        for k in range(1, nctx):
            at = lax.rem(me_x + k, nctx)
            pltpu.make_async_remote_copy(
                src_ref=slots.at[at],
                dst_ref=slots.at[at],
                send_sem=send.at[k],
                recv_sem=recv.at[at],
                device_id={"ctx": at},
                device_id_type=MESH,
            ).wait_recv()

    def iota(shape, dim):
        return lax.broadcasted_iota(jnp.int32, shape, dim)

    def column(row):
        size = row.shape[1]
        eye = iota((size, size), 0) == iota((size, size), 1)
        return jnp.sum(jnp.where(eye, jnp.broadcast_to(row, (size, size)), 0.0), axis=1, keepdims=True)

    for k in (4, 3, 5):
        loads[k].wait()
    middle = float(span // 2)
    rate = jnp.concatenate([decay_ref[g : g + 1, :] for g in range(groups)], axis=1)
    weight = jnp.concatenate([residue_ref[g : g + 1, :] for g in range(groups)], axis=1)
    root = jnp.sqrt(2.0 * rate)
    weight = weight * root
    rate_c, weight_c = column(rate), column(weight)
    from_middle = iota((lanes, span), 1).astype(F32) - middle
    falling = weight_c * jnp.exp(-rate_c * from_middle)
    rising = jnp.exp(rate_c * from_middle)
    row_group = lax.div(iota((lanes, span), 0), modes)
    lane_group = lax.div(iota((span, lanes), 1), modes)

    def wide(table):
        return jnp.concatenate(
            [jnp.where(row_group == g, table, 0.0) for g in range(groups)], axis=1
        ).astype(BF16)

    def tall(table):
        return jnp.concatenate(
            [jnp.where(lane_group == g, table, 0.0) for g in range(groups)], axis=0
        ).astype(BF16)

    def split(table):
        high = table.astype(BF16)
        return high, (table - high.astype(F32)).astype(BF16)

    rise_wide = wide(falling * jnp.exp(-rate_c * middle))
    fall_wide[...] = wide(weight_c * rising * jnp.exp(-rate_c * (span - 1.0 - middle)))
    from_middle_col = iota((span, lanes), 0).astype(F32) - middle
    fall_col = jnp.exp(-rate * from_middle_col)
    rise_col = jnp.exp(rate * from_middle_col)
    tail = tall(rise_col * jnp.exp(-rate * (span - middle)))
    decay_in = tall(fall_col * jnp.exp(-rate * middle))
    rise_col = rise_col.astype(BF16)

    loads[0].wait()
    loads[1].wait()

    def gate(n, carry):
        at = pl.ds(pl.multiple_of(n * span, span), span)
        gated = (first[:, at].astype(F32) * second[:, at].astype(F32)).astype(BF16)
        rows = pl.ds(pl.multiple_of(n * width, width), width)
        for g in range(groups):
            x_buf[rows, g * span : (g + 1) * span] = gated[g * width : (g + 1) * width]
        return carry

    lax.fori_loop(0, spans, gate, 0, unroll=8)

    state = dot(x_buf[...], tail)
    span_decay = jnp.exp(-rate * span)
    powers = jnp.exp(-rate * span * iota((spans, lanes), 0).astype(F32))
    run = jnp.zeros((width, lanes), F32)
    for n in range(spans):
        at = slice(n * width, (n + 1) * width)
        enter_buf[at, :] = run
        run = run * span_decay + state[at]
    fwd_slots[me_x] = run
    fwd_copies = spread(fwd_slots, fwd_send, fwd_recv)

    lower = iota((span, span), 0) >= iota((span, span), 1)
    fall_high, fall_low = split(falling)
    rise_high, rise_low = split(rising)
    for g in range(groups):
        at = slice(g * modes, (g + 1) * modes)
        toeplitz = dot_tn(
            jnp.concatenate([fall_high[at], fall_high[at], fall_low[at]], axis=0),
            jnp.concatenate([rise_high[at], rise_low[at], rise_high[at]], axis=0),
        )
        toep[g] = jnp.where(lower, toeplitz, 0.0).astype(BF16)
        at = slice(g * span, (g + 1) * span)
        conv[:, at] = dot_nt(x_buf[:, at], toep[g])
    for n in range(spans):
        power = jnp.broadcast_to(powers[n : n + 1], (width, lanes))
        fwd_pow[n * width : (n + 1) * width, :] = power
        bwd_pow[(spans - 1 - n) * width : (spans - n) * width, :] = power
    skip_wide = jnp.broadcast_to(column(skip_ref[...]), (channels, span))
    gather(fwd_slots, fwd_send, fwd_recv)

    def entering(slots, before):
        total = jnp.zeros((width, lanes), F32)
        for k in range(nctx):
            gap = me_x - 1 - k if before else k - 1 - me_x
            steps = jnp.maximum(gap, 0).astype(F32)
            decayed = slots[k] * jnp.exp(-rate * length * steps)
            total = total + jnp.where(gap >= 0, decayed, 0.0)
        return jnp.concatenate([total] * spans, axis=0)

    enter = enter_buf[...] + fwd_pow[...] * entering(fwd_slots, True)
    enter_buf[...] = enter
    conv[...] = conv[...] + dot(enter.astype(BF16), rise_wide)

    send_to(range(first_step, second_step))

    loads[2].wait()
    skip_sum = jnp.zeros((channels, span), F32)
    far_sum = jnp.zeros((width, lanes), F32)
    bwd_sum = jnp.zeros((width, lanes), F32)

    def over_spans(rows):
        total = rows[0:width]
        for at in range(width, rows.shape[0], width):
            total = total + rows[at : at + width]
        return total

    bwd_copies = []
    state_decay = jnp.exp(-rate)
    for k, (batch_units, place) in enumerate(batches):
        for p in range(batch_units):
            at_unit = flip(lax.div(me, per_unit), place * batch_units + p)
            for q in range(per_unit):
                src = at_unit * per_unit + q
                pltpu.make_async_copy(
                    heads_hbm.at[rows_of(0)], heads.at[:, cols_of(src)], recv_sem.at[src]
                ).wait()
            if p == 0 and k == min(2, len(batches) - 1):
                send_to(range(second_step, nch))
            for q in range(unit_spans):
                n = at_unit * unit_spans + q
                cols = pl.ds(pl.multiple_of(n * span, span), span)
                rows = pl.ds(pl.multiple_of(n * width, width), width)

                def stacked(ref):
                    return jnp.concatenate(
                        [ref[rows, g * span : (g + 1) * span] for g in range(groups)], axis=0
                    ).astype(F32)

                out_grad = heads[:, cols].astype(F32)
                grad = out_grad * third[:, cols].astype(F32)
                gated = stacked(x_buf)
                skip_sum = skip_sum + grad * gated
                convolved = stacked(conv) + skip_wide * gated
                stage_third[:, cols] = (out_grad * convolved).astype(BF16)
                rounded, direct = grad.astype(BF16), skip_wide * grad
                for g in range(groups):
                    at = slice(g * width, (g + 1) * width)
                    g_buf[rows, g * span : (g + 1) * span] = rounded[at]
                    conv[rows, g * span : (g + 1) * span] = direct[at]
        at_batch = flip(lax.div(me, per_unit * batch_units), place)
        batch_rows = batch_units * unit_spans * width
        rows = pl.ds(pl.multiple_of(at_batch * batch_rows, batch_rows), batch_rows)
        weighted = dot(g_buf[rows, :], decay_in)
        state = weighted * state_decay
        bwd_sum = bwd_sum + over_spans(state * fwd_pow[rows, :])
        if k == len(batches) - 1:
            bwd_slots[me_x] = bwd_sum
            bwd_copies = spread(bwd_slots, bwd_send, bwd_recv)
        leave_buf[rows, :] = state
        far_sum = far_sum + over_spans(weighted * enter_buf[rows, :])
        for g in range(groups):
            at = slice(g * span, (g + 1) * span)
            part = g_buf[rows, at]
            cross = dot_tn(part, x_buf[rows, at])
            cross_buf[g] = cross if k == 0 else cross_buf[g] + cross
            if k < len(batches) - 1:
                conv[rows, at] = conv[rows, at] + dot(part, toep[g])

    filter_sum = jnp.sum(far_sum, axis=0, keepdims=True)
    for g in range(groups):
        cross = jnp.where(lower, cross_buf[g], 0.0).astype(BF16)
        near = jnp.sum(dot(cross, rise_col) * fall_col, axis=0, keepdims=True)
        filter_sum = filter_sum + jnp.where(lane_group[0:1] == g, near, 0.0)
    skip_total = jnp.sum(skip_sum, axis=1, keepdims=True)
    eye = iota((channels, channels), 0) == iota((channels, channels), 1)
    sum_slots[me_x] = jnp.zeros(sum_slots.shape[1:], F32)
    sum_slots[me_x, 0:1, 0:lanes] = root * filter_sum
    sum_slots[me_x, 1:2, 0:channels] = jnp.sum(
        jnp.where(eye, jnp.broadcast_to(skip_total, (channels, channels)), 0.0),
        axis=0,
        keepdims=True,
    )
    sum_copies = spread(sum_slots, sum_send, sum_recv)
    for g in range(groups):
        at = slice(g * span, (g + 1) * span)
        conv[rows, at] = conv[rows, at] + dot(g_buf[rows, at], toep[g])
    run = jnp.zeros((width, lanes), F32)
    for n in reversed(range(spans)):
        at = slice(n * width, (n + 1) * width)
        state = leave_buf[at, :]
        leave_buf[at, :] = run
        run = run * span_decay + state

    gather(bwd_slots, bwd_send, bwd_recv)
    leave_buf[...] = leave_buf[...] + bwd_pow[...] * entering(bwd_slots, False)

    gather(sum_slots, sum_send, sum_recv)
    total = sum_slots[0]
    for k in range(1, nctx):
        total = total + sum_slots[k]
    for g in range(groups):
        out_residue[g : g + 1, :] = total[0:1, g * modes : (g + 1) * modes] / jnp.sqrt(
            F32(width * seq_total)
        )
    out_skip[...] = total[1:2, 0:channels] / jnp.sqrt(F32(seq_total))

    for copy in sends + fwd_copies + bwd_copies + sum_copies:
        copy.wait_send()


def finish(
    width,
    first, second, third, conv, leave, fall_wide, residue, skip,
    out_first, out_second, out_third, out_residue, out_skip,
    stage_first, stage_second, sem,
):
    channels, length = first.shape
    groups = channels // width
    span = conv.shape[1] // groups
    spans = length // span
    pieces = 4 if spans % 4 == 0 else 1
    piece_spans = spans // pieces
    copies = []

    def send(src, dst):
        copies.append(pltpu.make_async_copy(src, dst, sem.at[len(copies)]))
        copies[-1].start()

    for p in range(pieces):
        cols = pl.ds(p * piece_spans * span, piece_spans * span)
        send(third.at[:, cols], out_third.at[:, cols])
    send(residue, out_residue)
    send(skip, out_skip)
    for p in range(pieces):
        rows = slice(p * piece_spans * width, (p + 1) * piece_spans * width)
        for g in range(groups):
            lanes = slice(g * span, (g + 1) * span)
            mixed = conv[rows, lanes] + dot(leave[rows, :].astype(BF16), fall_wide[:, lanes])
            for q in range(piece_spans):
                n = p * piece_spans + q
                part = mixed[q * width : (q + 1) * width]
                at = (slice(g * width, (g + 1) * width), slice(n * span, (n + 1) * span))
                stage_first[at] = (part * second[at].astype(F32)).astype(BF16)
                stage_second[at] = (part * first[at].astype(F32)).astype(BF16)
        cols = pl.ds(p * piece_spans * span, piece_spans * span)
        send(stage_first.at[:, cols], out_first.at[:, cols])
        send(stage_second.at[:, cols], out_second.at[:, cols])
    for copy in copies:
        copy.wait()


def on_device(nch, nctx, first_in, second_in, third_in, grad_heads, residue, decay_rate, skip_gain):
    channels, length = first_in.shape
    groups, modes = residue.shape
    width = channels // groups
    span = min(256, length)
    rows = length // span * width
    lanes = groups * modes
    dims = (nch, nctx, channels, length, groups, modes, length * nctx)
    whole, vmem = pl.BlockSpec(memory_space=pltpu.HBM), pl.BlockSpec(memory_space=pltpu.VMEM)
    big = jax.ShapeDtypeStruct((channels, length), BF16)
    small = (
        jax.ShapeDtypeStruct((groups, modes), F32),
        jax.ShapeDtypeStruct((1, channels), F32),
    )
    big_buf = pltpu.VMEM((channels, length), BF16)
    half_buf = pltpu.VMEM((rows, groups * span), BF16)
    state_buf = pltpu.VMEM((rows, lanes), F32)
    slots = pltpu.VMEM((nctx, width, lanes), F32)
    dma = pltpu.SemaphoreType.DMA
    outs = pl.pallas_call(
        functools.partial(kernel, dims),
        out_shape=(
            big, big, big,
            jax.ShapeDtypeStruct((rows, groups * span), F32),
            jax.ShapeDtypeStruct((rows, lanes), F32),
            jax.ShapeDtypeStruct((lanes, groups * span), BF16),
            *small,
        ),
        in_specs=[whole] * 7,
        out_specs=[vmem] * 8,
        scratch_shapes=[
            big_buf, big_buf,
            half_buf, half_buf,
            pltpu.VMEM((groups, span, span), F32),
            pltpu.VMEM((groups, span, span), BF16),
            state_buf, state_buf, state_buf,
            slots, slots,
            pltpu.VMEM((nctx, 8, 128), F32),
            pltpu.VMEM((groups, modes), F32),
            pltpu.VMEM((groups, modes), F32),
            pltpu.VMEM((1, channels), F32),
            dma((6,)),
            dma((nch,)), dma((nch,)),
            dma((nctx,)), dma((nctx,)), dma((nctx,)), dma((nctx,)), dma((nctx,)), dma((nctx,)),
        ],
        compiler_params=pltpu.CompilerParams(
            collective_id=0, has_side_effects=True, vmem_limit_bytes=32 * 1024 * 1024
        ),
        cost_estimate=pl.CostEstimate(
            flops=12 * channels * length * span, bytes_accessed=14 * channels * length,
            transcendentals=0,
        ),
    )(
        *(
            pltpu.with_memory_space_constraint(part, pltpu.HBM)
            for part in (
                first_in, second_in, third_in, grad_heads, residue, decay_rate,
                skip_gain.reshape(1, channels),
            )
        )
    )
    outs = pl.pallas_call(
        functools.partial(finish, width),
        out_shape=(big, big, big, *small),
        in_specs=[vmem] * 8,
        out_specs=[whole] * 5,
        scratch_shapes=[big_buf, big_buf, dma((14,))],
        compiler_params=pltpu.CompilerParams(vmem_limit_bytes=16 * 1024 * 1024),
    )(*outs)
    return (*outs[:4], outs[4].reshape(channels))


def solution(mesh):
    return jax.shard_map(
        functools.partial(on_device, mesh.shape["ch"], mesh.shape["ctx"]),
        mesh=mesh,
        in_specs=(
            P("ch", "ctx"),
            P("ch", "ctx"),
            P("ch", "ctx"),
            P(None, ("ctx", "ch")),
            P("ch", None),
            P("ch", None),
            P("ch"),
        ),
        out_specs=(P("ch", "ctx"), P("ch", "ctx"), P("ch", "ctx"), P("ch", None), P("ch")),
        check_vma=False,
    )
```

```python
import functools

import jax
import jax.numpy as jnp
from jax import lax
from jax.experimental import pallas as pl
from jax.experimental.pallas import tpu as pltpu
from jax.sharding import PartitionSpec as P

MESH = pl.DeviceIdType.MESH
EXACT = lax.Precision.HIGHEST
F32 = jnp.float32
BF16 = jnp.bfloat16


def flip(index, bits):
    out, bit = index, 1
    while bit <= bits:
        if bits & bit:
            out = out + bit * (1 - 2 * lax.rem(lax.div(index, bit), 2))
        bit *= 2
    return out


def dot(a, b, precision=None):
    return jnp.dot(a, b, precision=precision, preferred_element_type=F32)


def dot_nt(a, b):
    return lax.dot_general(a, b, (((1,), (1,)), ((), ())), preferred_element_type=F32)


def dot_tn(a, b):
    return lax.dot_general(a, b, (((0,), (0,)), ((), ())), preferred_element_type=F32)


def kernel(
    dims,
    first_hbm, second_hbm, third_hbm, heads_hbm, residue_hbm, decay_hbm, skip_hbm,
    first, second, stage_third, conv, leave_buf, fall_wide, out_residue, out_skip,
    third, heads, x_buf, g_buf, cross_buf,
    toep, enter_buf, fwd_pow, bwd_pow, fwd_slots, bwd_slots, sum_slots,
    residue_ref, decay_ref, skip_ref,
    load_sem, send_sem, recv_sem, fwd_send, fwd_recv, bwd_send, bwd_recv, sum_send, sum_recv,
):
    nch, nctx, channels, length, groups, modes, seq_total = dims
    width = channels // groups
    chunk = length // nch
    span = min(256, length)
    spans = length // span
    lanes = groups * modes
    unit = max(chunk, span)
    per_unit = unit // chunk
    unit_spans = unit // span
    units = length // unit
    batches = [(units, 0)]
    if units % 8 == 0:
        batches = [(units // 4, k) for k in range(3)] + [(units // 8, 6), (units // 8, 7)]
    me = lax.axis_index("ch")
    me_x = lax.axis_index("ctx")

    loads = [
        pltpu.make_async_copy(src, dst, load_sem.at[k])
        for k, (src, dst) in enumerate(
            (
                (first_hbm, first),
                (second_hbm, second),
                (third_hbm, third),
                (residue_hbm, residue_ref),
                (decay_hbm, decay_ref),
                (skip_hbm, skip_ref),
            )
        )
    ]
    def rows_of(index):
        return pl.ds(pl.multiple_of(index * channels, channels), channels)

    own = pltpu.make_async_copy(
        heads_hbm.at[rows_of(me)], heads.at[me], recv_sem.at[me]
    )

    barrier = pltpu.get_barrier_semaphore()
    for s in range(1, nch):
        pl.semaphore_signal(barrier, inc=1, device_id={"ch": flip(me, s)}, device_id_type=MESH)
    for k in range(1, nctx):
        pl.semaphore_signal(
            barrier, inc=1, device_id={"ctx": lax.rem(me_x + k, nctx)}, device_id_type=MESH
        )
    for k in (4, 3, 5, 0, 1):
        loads[k].start()
    pl.semaphore_wait(barrier, nch - 1 + nctx - 1)

    sends = []

    def send_to(places):
        for s in places:
            to = flip(me, s)
            copy = pltpu.make_async_remote_copy(
                src_ref=heads_hbm.at[rows_of(to)],
                dst_ref=heads.at[me],
                send_sem=send_sem.at[s],
                recv_sem=recv_sem.at[me],
                device_id={"ch": to},
                device_id_type=MESH,
            )
            copy.start()
            sends.append(copy)

    send_to(range(nch // 2, nch * 3 // 4))
    send_to(range(1, nch // 2))
    own.start()
    loads[2].start()

    def spread(slots, send, recv):
        copies = []
        for k in range(1, nctx):
            copy = pltpu.make_async_remote_copy(
                src_ref=slots.at[me_x],
                dst_ref=slots.at[me_x],
                send_sem=send.at[k],
                recv_sem=recv.at[me_x],
                device_id={"ctx": lax.rem(me_x + k, nctx)},
                device_id_type=MESH,
            )
            copy.start()
            copies.append(copy)
        return copies

    def gather(slots, send, recv):
        for k in range(1, nctx):
            at = lax.rem(me_x + k, nctx)
            pltpu.make_async_remote_copy(
                src_ref=slots.at[at],
                dst_ref=slots.at[at],
                send_sem=send.at[k],
                recv_sem=recv.at[at],
                device_id={"ctx": at},
                device_id_type=MESH,
            ).wait_recv()

    def iota(shape, dim):
        return lax.broadcasted_iota(jnp.int32, shape, dim)

    def column(row):
        size = row.shape[1]
        eye = iota((size, size), 0) == iota((size, size), 1)
        return jnp.sum(jnp.where(eye, jnp.broadcast_to(row, (size, size)), 0.0), axis=1, keepdims=True)

    for k in (4, 3, 5):
        loads[k].wait()
    middle = float(span // 2)
    rate = jnp.concatenate([decay_ref[g : g + 1, :] for g in range(groups)], axis=1)
    weight = jnp.concatenate([residue_ref[g : g + 1, :] for g in range(groups)], axis=1)
    root = jnp.sqrt(2.0 * rate)
    weight = weight * root
    rate_c, weight_c = column(rate), column(weight)
    from_middle = iota((lanes, span), 1).astype(F32) - middle
    falling = weight_c * jnp.exp(-rate_c * from_middle)
    rising = jnp.exp(rate_c * from_middle)
    row_group = lax.div(iota((lanes, span), 0), modes)
    lane_group = lax.div(iota((span, lanes), 1), modes)

    def wide(table):
        return jnp.concatenate(
            [jnp.where(row_group == g, table, 0.0) for g in range(groups)], axis=1
        ).astype(BF16)

    def tall(table):
        return jnp.concatenate(
            [jnp.where(lane_group == g, table, 0.0) for g in range(groups)], axis=0
        ).astype(BF16)

    def split(table):
        high = table.astype(BF16)
        return high, (table - high.astype(F32)).astype(BF16)

    rise_wide = wide(falling * jnp.exp(-rate_c * middle))
    fall_wide[...] = wide(weight_c * rising * jnp.exp(-rate_c * (span - 1.0 - middle)))
    from_middle_col = iota((span, lanes), 0).astype(F32) - middle
    fall_col = jnp.exp(-rate * from_middle_col)
    rise_col = jnp.exp(rate * from_middle_col)
    tail = tall(rise_col * jnp.exp(-rate * (span - middle)))
    decay_in = tall(fall_col * jnp.exp(-rate * middle))
    rise_col = rise_col.astype(BF16)

    loads[0].wait()
    loads[1].wait()

    def gate(n, carry):
        at = pl.ds(pl.multiple_of(n * span, span), span)
        gated = (first[:, at].astype(F32) * second[:, at].astype(F32)).astype(BF16)
        rows = pl.ds(pl.multiple_of(n * width, width), width)
        for g in range(groups):
            x_buf[rows, g * span : (g + 1) * span] = gated[g * width : (g + 1) * width]
        return carry

    lax.fori_loop(0, spans, gate, 0, unroll=8)

    state = dot(x_buf[...], tail)
    span_decay = jnp.exp(-rate * span)
    powers = jnp.exp(-rate * span * iota((spans, lanes), 0).astype(F32))
    run = jnp.zeros((width, lanes), F32)
    for n in range(spans):
        at = slice(n * width, (n + 1) * width)
        enter_buf[at, :] = run
        run = run * span_decay + state[at]
    fwd_slots[me_x] = run
    fwd_copies = spread(fwd_slots, fwd_send, fwd_recv)

    lower = iota((span, span), 0) >= iota((span, span), 1)
    fall_high, fall_low = split(falling)
    rise_high, rise_low = split(rising)
    for g in range(groups):
        at = slice(g * modes, (g + 1) * modes)
        toeplitz = dot_tn(
            jnp.concatenate([fall_high[at], fall_high[at], fall_low[at]], axis=0),
            jnp.concatenate([rise_high[at], rise_low[at], rise_high[at]], axis=0),
        )
        toep[g] = jnp.where(lower, toeplitz, 0.0).astype(BF16)
        at = slice(g * span, (g + 1) * span)
        conv[:, at] = dot_nt(x_buf[:, at], toep[g])
    for n in range(spans):
        power = jnp.broadcast_to(powers[n : n + 1], (width, lanes))
        fwd_pow[n * width : (n + 1) * width, :] = power
        bwd_pow[(spans - 1 - n) * width : (spans - n) * width, :] = power
    skip_wide = jnp.broadcast_to(column(skip_ref[...]), (channels, span))
    gather(fwd_slots, fwd_send, fwd_recv)

    def entering(slots, before):
        total = jnp.zeros((width, lanes), F32)
        for k in range(nctx):
            gap = me_x - 1 - k if before else k - 1 - me_x
            steps = jnp.maximum(gap, 0).astype(F32)
            decayed = slots[k] * jnp.exp(-rate * length * steps)
            total = total + jnp.where(gap >= 0, decayed, 0.0)
        return jnp.concatenate([total] * spans, axis=0)

    enter = enter_buf[...] + fwd_pow[...] * entering(fwd_slots, True)
    enter_buf[...] = enter
    conv[...] = conv[...] + dot(enter.astype(BF16), rise_wide)

    send_to(range(nch * 3 // 4, nch))

    loads[2].wait()
    skip_sum = jnp.zeros((channels, span), F32)
    far_sum = jnp.zeros((width, lanes), F32)
    bwd_sum = jnp.zeros((width, lanes), F32)

    def over_spans(rows):
        total = rows[0:width]
        for at in range(width, rows.shape[0], width):
            total = total + rows[at : at + width]
        return total

    bwd_copies = []
    state_decay = jnp.exp(-rate)
    for k, (batch_units, place) in enumerate(batches):
        for p in range(batch_units):
            at_unit = flip(lax.div(me, per_unit), place * batch_units + p)
            for q in range(per_unit):
                src = at_unit * per_unit + q
                pltpu.make_async_copy(
                    heads_hbm.at[rows_of(0)], heads.at[src], recv_sem.at[src]
                ).wait()
            for q in range(unit_spans):
                n = at_unit * unit_spans + q
                cols = pl.ds(pl.multiple_of(n * span, span), span)
                rows = pl.ds(pl.multiple_of(n * width, width), width)

                def stacked(ref):
                    return jnp.concatenate(
                        [ref[rows, g * span : (g + 1) * span] for g in range(groups)], axis=0
                    ).astype(F32)

                if chunk >= span:
                    out_grad = heads[at_unit, :, q * span : (q + 1) * span].astype(F32)
                else:
                    out_grad = jnp.concatenate(
                        [heads[at_unit * per_unit + j] for j in range(per_unit)], axis=1
                    ).astype(F32)
                grad = out_grad * third[:, cols].astype(F32)
                gated = stacked(x_buf)
                skip_sum = skip_sum + grad * gated
                convolved = stacked(conv) + skip_wide * gated
                stage_third[:, cols] = (out_grad * convolved).astype(BF16)
                rounded, direct = grad.astype(BF16), skip_wide * grad
                for g in range(groups):
                    at = slice(g * width, (g + 1) * width)
                    g_buf[rows, g * span : (g + 1) * span] = rounded[at]
                    conv[rows, g * span : (g + 1) * span] = direct[at]
        at_batch = flip(lax.div(me, per_unit * batch_units), place)
        batch_rows = batch_units * unit_spans * width
        rows = pl.ds(pl.multiple_of(at_batch * batch_rows, batch_rows), batch_rows)
        weighted = dot(g_buf[rows, :], decay_in)
        state = weighted * state_decay
        bwd_sum = bwd_sum + over_spans(state * fwd_pow[rows, :])
        if k == len(batches) - 1:
            bwd_slots[me_x] = bwd_sum
            bwd_copies = spread(bwd_slots, bwd_send, bwd_recv)
        leave_buf[rows, :] = state
        far_sum = far_sum + over_spans(weighted * enter_buf[rows, :])
        for g in range(groups):
            at = slice(g * span, (g + 1) * span)
            part = g_buf[rows, at]
            cross = dot_tn(part, x_buf[rows, at])
            cross_buf[g] = cross if k == 0 else cross_buf[g] + cross
            if k < len(batches) - 1:
                conv[rows, at] = conv[rows, at] + dot(part, toep[g])

    filter_sum = jnp.sum(far_sum, axis=0, keepdims=True)
    for g in range(groups):
        cross = jnp.where(lower, cross_buf[g], 0.0).astype(BF16)
        near = jnp.sum(dot(cross, rise_col) * fall_col, axis=0, keepdims=True)
        filter_sum = filter_sum + jnp.where(lane_group[0:1] == g, near, 0.0)
    skip_total = jnp.sum(skip_sum, axis=1, keepdims=True)
    eye = iota((channels, channels), 0) == iota((channels, channels), 1)
    sum_slots[me_x] = jnp.zeros(sum_slots.shape[1:], F32)
    sum_slots[me_x, 0:1, 0:lanes] = root * filter_sum
    sum_slots[me_x, 1:2, 0:channels] = jnp.sum(
        jnp.where(eye, jnp.broadcast_to(skip_total, (channels, channels)), 0.0),
        axis=0,
        keepdims=True,
    )
    sum_copies = spread(sum_slots, sum_send, sum_recv)
    for g in range(groups):
        at = slice(g * span, (g + 1) * span)
        conv[rows, at] = conv[rows, at] + dot(g_buf[rows, at], toep[g])
    run = jnp.zeros((width, lanes), F32)
    for n in reversed(range(spans)):
        at = slice(n * width, (n + 1) * width)
        state = leave_buf[at, :]
        leave_buf[at, :] = run
        run = run * span_decay + state

    gather(bwd_slots, bwd_send, bwd_recv)
    leave_buf[...] = leave_buf[...] + bwd_pow[...] * entering(bwd_slots, False)

    gather(sum_slots, sum_send, sum_recv)
    total = sum_slots[0]
    for k in range(1, nctx):
        total = total + sum_slots[k]
    for g in range(groups):
        out_residue[g : g + 1, :] = total[0:1, g * modes : (g + 1) * modes] / jnp.sqrt(
            F32(width * seq_total)
        )
    out_skip[...] = total[1:2, 0:channels] / jnp.sqrt(F32(seq_total))

    for copy in sends + fwd_copies + bwd_copies + sum_copies:
        copy.wait_send()


def finish(
    width,
    first, second, third, conv, leave, fall_wide, residue, skip,
    out_first, out_second, out_third, out_residue, out_skip,
    stage_first, stage_second, sem,
):
    channels, length = first.shape
    groups = channels // width
    span = conv.shape[1] // groups
    spans = length // span
    pieces = 4 if spans % 4 == 0 else 1
    piece_spans = spans // pieces
    copies = []

    def send(src, dst):
        copies.append(pltpu.make_async_copy(src, dst, sem.at[len(copies)]))
        copies[-1].start()

    for p in range(pieces):
        cols = pl.ds(p * piece_spans * span, piece_spans * span)
        send(third.at[:, cols], out_third.at[:, cols])
    send(residue, out_residue)
    send(skip, out_skip)
    for p in range(pieces):
        rows = slice(p * piece_spans * width, (p + 1) * piece_spans * width)
        for g in range(groups):
            lanes = slice(g * span, (g + 1) * span)
            mixed = conv[rows, lanes] + dot(leave[rows, :].astype(BF16), fall_wide[:, lanes])
            for q in range(piece_spans):
                n = p * piece_spans + q
                part = mixed[q * width : (q + 1) * width]
                at = (slice(g * width, (g + 1) * width), slice(n * span, (n + 1) * span))
                stage_first[at] = (part * second[at].astype(F32)).astype(BF16)
                stage_second[at] = (part * first[at].astype(F32)).astype(BF16)
        cols = pl.ds(p * piece_spans * span, piece_spans * span)
        send(stage_first.at[:, cols], out_first.at[:, cols])
        send(stage_second.at[:, cols], out_second.at[:, cols])
    for copy in copies:
        copy.wait()


def on_device(nch, nctx, first_in, second_in, third_in, grad_heads, residue, decay_rate, skip_gain):
    channels, length = first_in.shape
    groups, modes = residue.shape
    width = channels // groups
    span = min(256, length)
    rows = length // span * width
    lanes = groups * modes
    dims = (nch, nctx, channels, length, groups, modes, length * nctx)
    whole, vmem = pl.BlockSpec(memory_space=pltpu.HBM), pl.BlockSpec(memory_space=pltpu.VMEM)
    big = jax.ShapeDtypeStruct((channels, length), BF16)
    small = (
        jax.ShapeDtypeStruct((groups, modes), F32),
        jax.ShapeDtypeStruct((1, channels), F32),
    )
    big_buf = pltpu.VMEM((channels, length), BF16)
    half_buf = pltpu.VMEM((rows, groups * span), BF16)
    state_buf = pltpu.VMEM((rows, lanes), F32)
    slots = pltpu.VMEM((nctx, width, lanes), F32)
    dma = pltpu.SemaphoreType.DMA
    outs = pl.pallas_call(
        functools.partial(kernel, dims),
        out_shape=(
            big, big, big,
            jax.ShapeDtypeStruct((rows, groups * span), F32),
            jax.ShapeDtypeStruct((rows, lanes), F32),
            jax.ShapeDtypeStruct((lanes, groups * span), BF16),
            *small,
        ),
        in_specs=[whole] * 7,
        out_specs=[vmem] * 8,
        scratch_shapes=[
            big_buf, pltpu.VMEM((nch, channels, length // nch), BF16),
            half_buf, half_buf,
            pltpu.VMEM((groups, span, span), F32),
            pltpu.VMEM((groups, span, span), BF16),
            state_buf, state_buf, state_buf,
            slots, slots,
            pltpu.VMEM((nctx, 8, 128), F32),
            pltpu.VMEM((groups, modes), F32),
            pltpu.VMEM((groups, modes), F32),
            pltpu.VMEM((1, channels), F32),
            dma((6,)),
            dma((nch,)), dma((nch,)),
            dma((nctx,)), dma((nctx,)), dma((nctx,)), dma((nctx,)), dma((nctx,)), dma((nctx,)),
        ],
        compiler_params=pltpu.CompilerParams(
            collective_id=0, has_side_effects=True, vmem_limit_bytes=32 * 1024 * 1024
        ),
        cost_estimate=pl.CostEstimate(
            flops=12 * channels * length * span, bytes_accessed=14 * channels * length,
            transcendentals=0,
        ),
    )(
        *(
            pltpu.with_memory_space_constraint(part, pltpu.HBM)
            for part in (
                first_in, second_in, third_in, grad_heads, residue, decay_rate,
                skip_gain.reshape(1, channels),
            )
        )
    )
    outs = pl.pallas_call(
        functools.partial(finish, width),
        out_shape=(big, big, big, *small),
        in_specs=[vmem] * 8,
        out_specs=[whole] * 5,
        scratch_shapes=[big_buf, big_buf, dma((14,))],
        compiler_params=pltpu.CompilerParams(vmem_limit_bytes=16 * 1024 * 1024),
    )(*outs)
    return (*outs[:4], outs[4].reshape(channels))


def solution(mesh):
    return jax.shard_map(
        functools.partial(on_device, mesh.shape["ch"], mesh.shape["ctx"]),
        mesh=mesh,
        in_specs=(
            P("ch", "ctx"),
            P("ch", "ctx"),
            P("ch", "ctx"),
            P(None, ("ctx", "ch")),
            P("ch", None),
            P("ch", None),
            P("ch"),
        ),
        out_specs=(P("ch", "ctx"), P("ch", "ctx"), P("ch", "ctx"), P("ch", None), P("ch")),
        check_vma=False,
    )
```

```python
import functools

import jax
import jax.numpy as jnp
from jax import lax
from jax.experimental import pallas as pl
from jax.experimental.pallas import tpu as pltpu
from jax.sharding import PartitionSpec as P

MESH = pl.DeviceIdType.MESH
EXACT = lax.Precision.HIGHEST
F32 = jnp.float32
BF16 = jnp.bfloat16


def flip(index, bits):
    out, bit = index, 1
    while bit <= bits:
        if bits & bit:
            out = out + bit * (1 - 2 * lax.rem(lax.div(index, bit), 2))
        bit *= 2
    return out


def interleaved(count):
    far, near = list(range(count // 2, count)), list(range(1, count // 2))
    order = []
    for k in range(len(far)):
        order.append(far[k])
        if k < len(near):
            order.append(near[k])
    return order


def dot(a, b, precision=None):
    return jnp.dot(a, b, precision=precision, preferred_element_type=F32)


def dot_nt(a, b):
    return lax.dot_general(a, b, (((1,), (1,)), ((), ())), preferred_element_type=F32)


def dot_tn(a, b):
    return lax.dot_general(a, b, (((0,), (0,)), ((), ())), preferred_element_type=F32)


def kernel(
    dims,
    first_hbm, second_hbm, third_hbm, heads_hbm, residue_hbm, decay_hbm, skip_hbm,
    first, second, stage_third, conv, leave_buf, fall_wide, out_residue, out_skip,
    third, heads, x_buf, g_buf, cross_buf,
    toep, toep_low, enter_buf, fwd_pow, bwd_pow, fwd_slots, bwd_slots, sum_slots,
    residue_ref, decay_ref, skip_ref,
    load_sem, send_sem, recv_sem, fwd_send, fwd_recv, bwd_send, bwd_recv, sum_send, sum_recv,
):
    nch, nctx, channels, length, groups, modes, seq_total = dims
    width = channels // groups
    chunk = length // nch
    span = min(256, length)
    spans = length // span
    lanes = groups * modes
    unit = max(chunk, span)
    per_unit = unit // chunk
    unit_spans = unit // span
    units = length // unit
    batches = [(units, 0)]
    if units % 8 == 0:
        batches = [(units // 4, k) for k in range(3)] + [(units // 8, 6), (units // 8, 7)]
    me = lax.axis_index("ch")
    me_x = lax.axis_index("ctx")

    loads = [
        pltpu.make_async_copy(src, dst, load_sem.at[k])
        for k, (src, dst) in enumerate(
            (
                (first_hbm, first),
                (second_hbm, second),
                (third_hbm, third),
                (residue_hbm, residue_ref),
                (decay_hbm, decay_ref),
                (skip_hbm, skip_ref),
            )
        )
    ]
    def rows_of(index):
        return pl.ds(pl.multiple_of(index * channels, channels), channels)

    own = pltpu.make_async_copy(
        heads_hbm.at[rows_of(me)], heads.at[me], recv_sem.at[me]
    )

    barrier = pltpu.get_barrier_semaphore()
    for s in range(1, nch):
        pl.semaphore_signal(barrier, inc=1, device_id={"ch": flip(me, s)}, device_id_type=MESH)
    for k in range(1, nctx):
        pl.semaphore_signal(
            barrier, inc=1, device_id={"ctx": lax.rem(me_x + k, nctx)}, device_id_type=MESH
        )
    for k in (4, 3, 5, 0, 1):
        loads[k].start()
    pl.semaphore_wait(barrier, nch - 1 + nctx - 1)

    sends = []

    def send_to(places):
        for s in places:
            to = flip(me, s)
            copy = pltpu.make_async_remote_copy(
                src_ref=heads_hbm.at[rows_of(to)],
                dst_ref=heads.at[me],
                send_sem=send_sem.at[s],
                recv_sem=recv_sem.at[me],
                device_id={"ch": to},
                device_id_type=MESH,
            )
            copy.start()
            sends.append(copy)

    send_to(interleaved(nch))
    own.start()
    loads[2].start()

    def spread(slots, send, recv):
        copies = []
        for k in range(1, nctx):
            copy = pltpu.make_async_remote_copy(
                src_ref=slots.at[me_x],
                dst_ref=slots.at[me_x],
                send_sem=send.at[k],
                recv_sem=recv.at[me_x],
                device_id={"ctx": lax.rem(me_x + k, nctx)},
                device_id_type=MESH,
            )
            copy.start()
            copies.append(copy)
        return copies

    def gather(slots, send, recv):
        for k in range(1, nctx):
            at = lax.rem(me_x + k, nctx)
            pltpu.make_async_remote_copy(
                src_ref=slots.at[at],
                dst_ref=slots.at[at],
                send_sem=send.at[k],
                recv_sem=recv.at[at],
                device_id={"ctx": at},
                device_id_type=MESH,
            ).wait_recv()

    def iota(shape, dim):
        return lax.broadcasted_iota(jnp.int32, shape, dim)

    def column(row):
        size = row.shape[1]
        eye = iota((size, size), 0) == iota((size, size), 1)
        return jnp.sum(jnp.where(eye, jnp.broadcast_to(row, (size, size)), 0.0), axis=1, keepdims=True)

    for k in (4, 3, 5):
        loads[k].wait()
    middle = float(span // 2)
    rate = jnp.concatenate([decay_ref[g : g + 1, :] for g in range(groups)], axis=1)
    weight = jnp.concatenate([residue_ref[g : g + 1, :] for g in range(groups)], axis=1)
    root = jnp.sqrt(2.0 * rate)
    weight = weight * root
    rate_c, weight_c = column(rate), column(weight)
    from_middle = iota((lanes, span), 1).astype(F32) - middle
    falling = weight_c * jnp.exp(-rate_c * from_middle)
    rising = jnp.exp(rate_c * from_middle)
    row_group = lax.div(iota((lanes, span), 0), modes)
    lane_group = lax.div(iota((span, lanes), 1), modes)

    def wide(table):
        return jnp.concatenate(
            [jnp.where(row_group == g, table, 0.0) for g in range(groups)], axis=1
        )

    def tall(table):
        return jnp.concatenate(
            [jnp.where(lane_group == g, table, 0.0) for g in range(groups)], axis=0
        )

    def split(table):
        high = table.astype(BF16)
        return high, (table - high.astype(F32)).astype(BF16)

    rise_wide, rise_wide_low = split(wide(falling * jnp.exp(-rate_c * middle)))
    fall_wide[...] = wide(weight_c * rising * jnp.exp(-rate_c * (span - 1.0 - middle))).astype(BF16)
    from_middle_col = iota((span, lanes), 0).astype(F32) - middle
    fall_col = jnp.exp(-rate * from_middle_col)
    rise_col = jnp.exp(rate * from_middle_col)
    tail, tail_low = split(tall(rise_col * jnp.exp(-rate * (span - middle))))
    decay_in, decay_in_low = split(tall(fall_col * jnp.exp(-rate * middle)))
    rise_col = rise_col.astype(BF16)

    loads[0].wait()
    loads[1].wait()

    def gate(n, carry):
        at = pl.ds(pl.multiple_of(n * span, span), span)
        gated = (first[:, at].astype(F32) * second[:, at].astype(F32)).astype(BF16)
        rows = pl.ds(pl.multiple_of(n * width, width), width)
        for g in range(groups):
            x_buf[rows, g * span : (g + 1) * span] = gated[g * width : (g + 1) * width]
        return carry

    lax.fori_loop(0, spans, gate, 0, unroll=8)

    state = dot(x_buf[...], tail) + dot(x_buf[...], tail_low)
    span_decay = jnp.exp(-rate * span)
    powers = jnp.exp(-rate * span * iota((spans, lanes), 0).astype(F32))
    run = jnp.zeros((width, lanes), F32)
    for n in range(spans):
        at = slice(n * width, (n + 1) * width)
        enter_buf[at, :] = run
        run = run * span_decay + state[at]
    fwd_slots[me_x] = run
    fwd_copies = spread(fwd_slots, fwd_send, fwd_recv)

    lower = iota((span, span), 0) >= iota((span, span), 1)
    fall_high, fall_low = split(falling)
    rise_high, rise_low = split(rising)
    for g in range(groups):
        at = slice(g * modes, (g + 1) * modes)
        toeplitz = dot_tn(
            jnp.concatenate([fall_high[at], fall_high[at], fall_low[at]], axis=0),
            jnp.concatenate([rise_high[at], rise_low[at], rise_high[at]], axis=0),
        )
        toep[g], toep_low[g] = split(jnp.where(lower, toeplitz, 0.0))
        at = slice(g * span, (g + 1) * span)
        conv[:, at] = dot_nt(x_buf[:, at], toep[g]) + dot_nt(x_buf[:, at], toep_low[g])
    for n in range(spans):
        power = jnp.broadcast_to(powers[n : n + 1], (width, lanes))
        fwd_pow[n * width : (n + 1) * width, :] = power
        bwd_pow[(spans - 1 - n) * width : (spans - n) * width, :] = power
    skip_wide = jnp.broadcast_to(column(skip_ref[...]), (channels, span))
    gather(fwd_slots, fwd_send, fwd_recv)

    def entering(slots, before):
        total = jnp.zeros((width, lanes), F32)
        for k in range(nctx):
            gap = me_x - 1 - k if before else k - 1 - me_x
            steps = jnp.maximum(gap, 0).astype(F32)
            decayed = slots[k] * jnp.exp(-rate * length * steps)
            total = total + jnp.where(gap >= 0, decayed, 0.0)
        return jnp.concatenate([total] * spans, axis=0)

    enter = enter_buf[...] + fwd_pow[...] * entering(fwd_slots, True)
    enter_buf[...] = enter
    enter, enter_low = split(enter)
    conv[...] = (
        conv[...] + dot(enter, rise_wide) + dot(enter_low, rise_wide) + dot(enter, rise_wide_low)
    )

    loads[2].wait()
    skip_sum = jnp.zeros((channels, span), F32)
    far_sum = jnp.zeros((width, lanes), F32)
    bwd_sum = jnp.zeros((width, lanes), F32)

    def over_spans(rows):
        total = rows[0:width]
        for at in range(width, rows.shape[0], width):
            total = total + rows[at : at + width]
        return total

    bwd_copies = []
    state_decay = jnp.exp(-rate)
    for k, (batch_units, place) in enumerate(batches):
        for p in range(batch_units):
            at_unit = flip(lax.div(me, per_unit), place * batch_units + p)
            for q in range(per_unit):
                src = at_unit * per_unit + q
                pltpu.make_async_copy(
                    heads_hbm.at[rows_of(0)], heads.at[src], recv_sem.at[src]
                ).wait()
            for q in range(unit_spans):
                n = at_unit * unit_spans + q
                cols = pl.ds(pl.multiple_of(n * span, span), span)
                rows = pl.ds(pl.multiple_of(n * width, width), width)

                def stacked(ref):
                    return jnp.concatenate(
                        [ref[rows, g * span : (g + 1) * span] for g in range(groups)], axis=0
                    ).astype(F32)

                if chunk >= span:
                    out_grad = heads[at_unit, :, q * span : (q + 1) * span].astype(F32)
                else:
                    out_grad = jnp.concatenate(
                        [heads[at_unit * per_unit + j] for j in range(per_unit)], axis=1
                    ).astype(F32)
                grad = out_grad * third[:, cols].astype(F32)
                gated = stacked(x_buf)
                skip_sum = skip_sum + grad * gated
                convolved = stacked(conv) + skip_wide * gated
                stage_third[:, cols] = (out_grad * convolved).astype(BF16)
                rounded, direct = grad.astype(BF16), skip_wide * grad
                for g in range(groups):
                    at = slice(g * width, (g + 1) * width)
                    g_buf[rows, g * span : (g + 1) * span] = rounded[at]
                    conv[rows, g * span : (g + 1) * span] = direct[at]
        at_batch = flip(lax.div(me, per_unit * batch_units), place)
        batch_rows = batch_units * unit_spans * width
        rows = pl.ds(pl.multiple_of(at_batch * batch_rows, batch_rows), batch_rows)
        weighted = dot(g_buf[rows, :], decay_in) + dot(g_buf[rows, :], decay_in_low)
        state = weighted * state_decay
        bwd_sum = bwd_sum + over_spans(state * fwd_pow[rows, :])
        if k == len(batches) - 1:
            bwd_slots[me_x] = bwd_sum
            bwd_copies = spread(bwd_slots, bwd_send, bwd_recv)
        leave_buf[rows, :] = state
        far_sum = far_sum + over_spans(weighted * enter_buf[rows, :])
        for g in range(groups):
            at = slice(g * span, (g + 1) * span)
            part = g_buf[rows, at]
            cross = dot_tn(part, x_buf[rows, at])
            cross_buf[g] = cross if k == 0 else cross_buf[g] + cross
            if k < len(batches) - 1:
                conv[rows, at] = conv[rows, at] + dot(part, toep[g]) + dot(part, toep_low[g])

    filter_sum = jnp.sum(far_sum, axis=0, keepdims=True)
    for g in range(groups):
        cross = jnp.where(lower, cross_buf[g], 0.0).astype(BF16)
        near = jnp.sum(dot(cross, rise_col) * fall_col, axis=0, keepdims=True)
        filter_sum = filter_sum + jnp.where(lane_group[0:1] == g, near, 0.0)
    skip_total = jnp.sum(skip_sum, axis=1, keepdims=True)
    eye = iota((channels, channels), 0) == iota((channels, channels), 1)
    sum_slots[me_x] = jnp.zeros(sum_slots.shape[1:], F32)
    sum_slots[me_x, 0:1, 0:lanes] = root * filter_sum
    sum_slots[me_x, 1:2, 0:channels] = jnp.sum(
        jnp.where(eye, jnp.broadcast_to(skip_total, (channels, channels)), 0.0),
        axis=0,
        keepdims=True,
    )
    sum_copies = spread(sum_slots, sum_send, sum_recv)
    for g in range(groups):
        at = slice(g * span, (g + 1) * span)
        conv[rows, at] = conv[rows, at] + dot(g_buf[rows, at], toep[g])
    run = jnp.zeros((width, lanes), F32)
    for n in reversed(range(spans)):
        at = slice(n * width, (n + 1) * width)
        state = leave_buf[at, :]
        leave_buf[at, :] = run
        run = run * span_decay + state

    gather(bwd_slots, bwd_send, bwd_recv)
    leave_buf[...] = leave_buf[...] + bwd_pow[...] * entering(bwd_slots, False)

    gather(sum_slots, sum_send, sum_recv)
    total = sum_slots[0]
    for k in range(1, nctx):
        total = total + sum_slots[k]
    for g in range(groups):
        out_residue[g : g + 1, :] = total[0:1, g * modes : (g + 1) * modes] / jnp.sqrt(
            F32(width * seq_total)
        )
    out_skip[...] = total[1:2, 0:channels] / jnp.sqrt(F32(seq_total))

    for copy in sends + fwd_copies + bwd_copies + sum_copies:
        copy.wait_send()


def finish(
    width,
    first, second, third, conv, leave, fall_wide, residue, skip,
    out_first, out_second, out_third, out_residue, out_skip,
    stage_first, stage_second, sem,
):
    channels, length = first.shape
    groups = channels // width
    span = conv.shape[1] // groups
    spans = length // span
    pieces = 8 if spans % 8 == 0 else 1
    piece_spans = spans // pieces
    copies = []

    def send(src, dst):
        copies.append(pltpu.make_async_copy(src, dst, sem.at[len(copies)]))
        copies[-1].start()

    quarter = length // 4
    for p in range(4):
        cols = pl.ds(p * quarter, quarter)
        send(third.at[:, cols], out_third.at[:, cols])
    send(residue, out_residue)
    send(skip, out_skip)
    for p in range(pieces):
        rows = slice(p * piece_spans * width, (p + 1) * piece_spans * width)
        for g in range(groups):
            lanes = slice(g * span, (g + 1) * span)
            mixed = conv[rows, lanes] + dot(leave[rows, :].astype(BF16), fall_wide[:, lanes])
            for q in range(piece_spans):
                n = p * piece_spans + q
                part = mixed[q * width : (q + 1) * width]
                at = (slice(g * width, (g + 1) * width), slice(n * span, (n + 1) * span))
                stage_first[at] = (part * second[at].astype(F32)).astype(BF16)
                stage_second[at] = (part * first[at].astype(F32)).astype(BF16)
        cols = pl.ds(p * piece_spans * span, piece_spans * span)
        send(stage_first.at[:, cols], out_first.at[:, cols])
        send(stage_second.at[:, cols], out_second.at[:, cols])
    for copy in copies:
        copy.wait()


def on_device(nch, nctx, first_in, second_in, third_in, grad_heads, residue, decay_rate, skip_gain):
    channels, length = first_in.shape
    groups, modes = residue.shape
    width = channels // groups
    span = min(256, length)
    rows = length // span * width
    lanes = groups * modes
    dims = (nch, nctx, channels, length, groups, modes, length * nctx)
    whole, vmem = pl.BlockSpec(memory_space=pltpu.HBM), pl.BlockSpec(memory_space=pltpu.VMEM)
    big = jax.ShapeDtypeStruct((channels, length), BF16)
    small = (
        jax.ShapeDtypeStruct((groups, modes), F32),
        jax.ShapeDtypeStruct((1, channels), F32),
    )
    big_buf = pltpu.VMEM((channels, length), BF16)
    half_buf = pltpu.VMEM((rows, groups * span), BF16)
    state_buf = pltpu.VMEM((rows, lanes), F32)
    slots = pltpu.VMEM((nctx, width, lanes), F32)
    dma = pltpu.SemaphoreType.DMA
    outs = pl.pallas_call(
        functools.partial(kernel, dims),
        out_shape=(
            big, big, big,
            jax.ShapeDtypeStruct((rows, groups * span), F32),
            jax.ShapeDtypeStruct((rows, lanes), F32),
            jax.ShapeDtypeStruct((lanes, groups * span), BF16),
            *small,
        ),
        in_specs=[whole] * 7,
        out_specs=[vmem] * 8,
        scratch_shapes=[
            big_buf, pltpu.VMEM((nch, channels, length // nch), BF16),
            half_buf, half_buf,
            pltpu.VMEM((groups, span, span), F32),
            pltpu.VMEM((groups, span, span), BF16),
            pltpu.VMEM((groups, span, span), BF16),
            state_buf, state_buf, state_buf,
            slots, slots,
            pltpu.VMEM((nctx, 8, 128), F32),
            pltpu.VMEM((groups, modes), F32),
            pltpu.VMEM((groups, modes), F32),
            pltpu.VMEM((1, channels), F32),
            dma((6,)),
            dma((nch,)), dma((nch,)),
            dma((nctx,)), dma((nctx,)), dma((nctx,)), dma((nctx,)), dma((nctx,)), dma((nctx,)),
        ],
        compiler_params=pltpu.CompilerParams(
            collective_id=0, has_side_effects=True, vmem_limit_bytes=32 * 1024 * 1024
        ),
        cost_estimate=pl.CostEstimate(
            flops=12 * channels * length * span, bytes_accessed=14 * channels * length,
            transcendentals=0,
        ),
    )(
        *(
            pltpu.with_memory_space_constraint(part, pltpu.HBM)
            for part in (
                first_in, second_in, third_in, grad_heads, residue, decay_rate,
                skip_gain.reshape(1, channels),
            )
        )
    )
    outs = pl.pallas_call(
        functools.partial(finish, width),
        out_shape=(big, big, big, *small),
        in_specs=[vmem] * 8,
        out_specs=[whole] * 5,
        scratch_shapes=[big_buf, big_buf, dma((22,))],
        compiler_params=pltpu.CompilerParams(vmem_limit_bytes=16 * 1024 * 1024),
    )(*outs)
    return (*outs[:4], outs[4].reshape(channels))


def solution(mesh):
    return jax.shard_map(
        functools.partial(on_device, mesh.shape["ch"], mesh.shape["ctx"]),
        mesh=mesh,
        in_specs=(
            P("ch", "ctx"),
            P("ch", "ctx"),
            P("ch", "ctx"),
            P(None, ("ctx", "ch")),
            P("ch", None),
            P("ch", None),
            P("ch"),
        ),
        out_specs=(P("ch", "ctx"), P("ch", "ctx"), P("ch", "ctx"), P("ch", None), P("ch")),
        check_vma=False,
    )
```
